256 devices in a mesh: tm: 16 (over x_hi, y, core), rows: 16 (over x_lo, z).
Axes of the slice: x: 4 (x_hi: 2, x_lo: 2; x = x_hi * 2 + x_lo), y: 4, z: 8, core: 2. Of those that a mesh axis runs over, the one named last changes fastest.
Arguments:
- snapshots: bfloat16 [32768, 32768], P('tm', 'rows'), may hold values from -6 to 6
- spod_modes: bfloat16 [64, 2, 4, 32768], P('tm', None, None, 'rows'), may hold values from -0.046875 to 0.046875
- freq_index: int32 [64], replicated, may hold values from 1 to 128, as said below
- seg_offsets: int32 [8192], P('tm'), may hold values from 0 to 2047, as said below
Outputs:
- coefficients: float32 [64, 2, 4, 8192], P('rows', None, None, 'tm')
The draws below stay inside these ranges and needn't reach their ends.
Inputs may be any that keep to these rules, and one draw needn't show every extreme that they name: Frequency f is bin freq_index[f] of a segment of 256 snapshots; values may repeat. Segment n starts at snapshot (n // 512) * 2048 + seg_offsets[n]; snapshots past the last one count as zeros.
All inputs are finite; a program needn't handle non-finite values.
Results may differ from the reference program's by a relative error of at most 0.0003.
Values may be sent and summed in bfloat16 or wider, within the bound.
A program may use at most 64 MiB of HBM per device.

```python
import math
import jax
import jax.numpy as jnp
from jax import lax

F = 64
M = 4
L = 256
T_DEV = 2048
S_DEV = 512
NT = 32768
NR = 32768
NSEG = 8192
N_TM = 16


def force_ends(key, length, block_len, lowest, highest):
    drawn = jax.random.randint(jax.random.fold_in(key, 1), (length,), lowest, highest + 1, dtype=jnp.int32)
    blocks = length // block_len
    high_pos = jax.random.randint(jax.random.fold_in(key, 2), (blocks,), 0, block_len, dtype=jnp.int32)
    step_pos = jax.random.randint(jax.random.fold_in(key, 3), (blocks,), 0, block_len - 1, dtype=jnp.int32)
    low_pos = (high_pos + 1 + step_pos) % block_len
    positions = jnp.arange(length, dtype=jnp.int32)
    within = positions % block_len
    owners = positions // block_len
    result = jnp.where(within == high_pos[owners], highest, drawn)
    return jnp.where(within == low_pos[owners], lowest, result).astype(jnp.int32)


def draw_freq_index(key, part):
    return force_ends(jax.random.fold_in(key, 11), F, F, 1, L // 2)


def draw_seg_offsets(key, part):
    return force_ends(jax.random.fold_in(key, 23), NSEG, S_DEV, 0, T_DEV - 1)


def with_spikes(entries, key, source, target, blocks, factor):
    owner, partner = [(jnp.arange(entries.shape[dim]) // (entries.shape[dim] // blocks)).reshape([-1 if axis == dim else 1 for axis in range(entries.ndim)]) for dim in (source, target)]
    chosen = jax.random.permutation(key, blocks)[partner]
    strong = (owner == chosen) | (owner == (partner + blocks // 2) % blocks)
    return jnp.where(strong, factor * entries, entries)


def levels(own_key, dims, shards, low, top_value):
    def one(axis_at, parts):
        steps = jax.random.uniform(jax.random.fold_in(jax.random.fold_in(own_key, 6), axis_at), (parts,), jnp.float32, low / len(shards), top_value / len(shards))
        return jnp.repeat(jnp.exp(steps), dims[axis_at] // parts).reshape((-1,) + (1,) * (len(dims) - axis_at - 1))

    loudness = one(*shards[0])
    for cut in shards[1:]:
        loudness = loudness * one(*cut)
    return loudness


def normal_values(stream_key, shape, deviation, reach, cuts=(), kind=jnp.bfloat16):
    gain = levels(stream_key, shape, cuts, -0.22, 0.18) if cuts else 1.0
    entries = jax.random.normal(stream_key, shape, jnp.float32) * deviation * gain
    return jnp.minimum(jnp.maximum(entries, -reach), reach).astype(kind)


def gaussian_with(rng, extent, deviation, most, shards, heavy, kind=jnp.bfloat16):
    values = deviation * jax.random.normal(rng, extent, jnp.float32)
    if shards:
        values = values * levels(rng, extent, shards, -0.22, 0.18)
    return jnp.clip(with_spikes(values, jax.random.fold_in(rng, 3), *heavy), -most, most).astype(kind)


def setup_inputs(seed: int = 0) -> dict:
    seeds = jax.random.split(jax.random.key(seed), 5)
    return {
        "snapshots": normal_values(seeds[0], (NT, NR), 1.0, 6.0, ((0, 16), (1, 16))),
        "spod_modes": gaussian_with(seeds[1], (F, 2, M, NR), NR ** -0.5, 0.046875, ((0, 16), (3, 16)), (3, 0, 16, 2.0)),
        "freq_index": draw_freq_index(jax.random.fold_in(seeds[4], 71), 0),
        "seg_offsets": draw_seg_offsets(jax.random.fold_in(seeds[4], 71), 0),
    }


def hann_weights(distance):
    inside = (distance >= 0) & (distance < L)
    angles = distance.astype(jnp.float32) * (2.0 * math.pi / L)
    values = math.sqrt(8.0 / (3.0 * L)) * (0.5 - 0.5 * jnp.cos(angles))
    return jnp.where(inside, values, 0.0).astype(jnp.float32)

def phase_pair(frequency, moments):
    phase_bin = frequency[:, None] * moments[None, :] % L
    angles = phase_bin.astype(jnp.float32) * (2.0 * math.pi / L)
    return (jnp.cos(angles)[:, None, :], jnp.sin(angles)[:, None, :])

def demodulate(projected, frequency, moments):
    cosine, sine_part = phase_pair(frequency, moments)
    real_in = projected[:, 0]
    imag_in = projected[:, 1]
    real_out = cosine * real_in - sine_part * imag_in
    imag_out = -(sine_part * real_in + cosine * imag_in)
    return jnp.stack([real_out, imag_out], 1).astype(jnp.float32)

def envelope(extended, offsets, frequency, base_time):
    distance = jnp.arange(extended.shape[3], dtype=jnp.int32)[None, :] - offsets[:, None]
    weights = hann_weights(distance)
    groups = extended.shape[0]
    flat_rows = extended.reshape(groups * extended.shape[1] * extended.shape[2], extended.shape[3])
    summed = lax.dot_general(flat_rows, weights, (((1,), (1,)), ((), ())), precision=lax.Precision.HIGHEST, preferred_element_type=jnp.float32)
    summed = summed.reshape(groups, 2, extended.shape[2], offsets.shape[0])
    cosine, sine_part = phase_pair(frequency, base_time + offsets)
    env_real = summed[:, 0]
    env_imag = summed[:, 1]
    return jnp.stack([cosine * env_real - sine_part * env_imag, sine_part * env_real + cosine * env_imag], 1)

def reference(snapshots, spod_modes, freq_index, seg_offsets):
    flat_modes = spod_modes.reshape(F * 2 * M, NR)
    projected = lax.dot_general(flat_modes, snapshots, (((1,), (1,)), ((), ())), preferred_element_type=jnp.float32)
    projected = projected.reshape(F, 2, M, NT)
    demodulated = demodulate(projected, freq_index, jnp.arange(NT, dtype=jnp.int32))
    padded = jnp.concatenate([demodulated, jnp.zeros((F, 2, M, L), jnp.float32)], 3)

    def one_block(block_id):
        extended = lax.dynamic_slice_in_dim(padded, (block_id * T_DEV).astype(jnp.int32), T_DEV + L, 3)
        offsets = lax.dynamic_slice_in_dim(seg_offsets, (block_id * S_DEV).astype(jnp.int32), S_DEV, 0)
        return envelope(extended, offsets, freq_index, (block_id * T_DEV).astype(jnp.int32))
    blocks = lax.map(one_block, jnp.arange(N_TM, dtype=jnp.int32))
    return jnp.moveaxis(blocks, 0, 3).reshape(F, 2, M, NSEG)
```

```python
import math

import jax
import jax.numpy as jnp
from jax import lax
from jax.sharding import PartitionSpec as P

F = 64
M = 4
L = 256


def hann_weights(distance):
    inside = (distance >= 0) & (distance < L)
    angles = distance.astype(jnp.float32) * (2.0 * math.pi / L)
    values = math.sqrt(8.0 / (3.0 * L)) * (0.5 - 0.5 * jnp.cos(angles))
    return jnp.where(inside, values, 0.0)


def phase_pair(frequency, moments):
    phase_bin = frequency[:, None] * moments[None, :] % L
    angles = phase_bin.astype(jnp.float32) * (2.0 * math.pi / L)
    return (jnp.cos(angles)[:, None, :], jnp.sin(angles)[:, None, :])


def demodulate(projected, frequency, moments):
    cosine, sine_part = phase_pair(frequency, moments)
    real_in = projected[:, 0]
    imag_in = projected[:, 1]
    real_out = cosine * real_in - sine_part * imag_in
    imag_out = -(sine_part * real_in + cosine * imag_in)
    return jnp.stack([real_out, imag_out], 1)


def body(snapshots, spod_modes, freq_index, seg_offsets):
    time_len = snapshots.shape[0]
    tm_pos = lax.axis_index("tm")
    row_pos = lax.axis_index("rows")
    block_rows = lax.all_gather(spod_modes, "tm", axis=0, tiled=True)
    flat_modes = block_rows.reshape(F * 2 * M, block_rows.shape[3])
    partial = lax.dot_general(
        flat_modes, snapshots, (((1,), (1,)), ((), ())), preferred_element_type=jnp.float32
    )
    route = [(i + 1, i) for i in range(lax.axis_size("tm") - 1)]
    behind = lax.ppermute(partial[:, :L], "tm", route)
    moments = tm_pos * time_len + jnp.arange(time_len + L, dtype=jnp.int32)

    def windowed(part, first, length):
        shaped = part.reshape(F, 2, M, length)
        demodulated = demodulate(shaped, freq_index, moments[first:first + length])
        at = first + jnp.arange(length, dtype=jnp.int32)
        weights = hann_weights(at[:, None] - seg_offsets[None, :])
        return lax.dot_general(
            demodulated.reshape(F * 2 * M, length),
            weights,
            (((1,), (0,)), ((), ())),
            precision=lax.Precision.HIGH,
            preferred_element_type=jnp.float32,
        )

    summed = windowed(partial, 0, time_len) + windowed(behind, time_len, L)
    summed = summed.reshape(F, 2, M, seg_offsets.shape[0])
    mine = lax.psum_scatter(summed, "rows", scatter_dimension=0, tiled=True)
    share_len = F // lax.axis_size("rows")
    own_freqs = lax.dynamic_slice_in_dim(freq_index, row_pos * share_len, share_len, 0)
    cosine, sine_part = phase_pair(own_freqs, tm_pos * time_len + seg_offsets)
    env_real = mine[:, 0]
    env_imag = mine[:, 1]
    return jnp.stack(
        [cosine * env_real - sine_part * env_imag, sine_part * env_real + cosine * env_imag], 1
    )


def solution(mesh):
    placed = (P("tm", "rows"), P("tm", None, None, "rows"), P(), P("tm"))
    return jax.shard_map(
        body, mesh=mesh, in_specs=placed, out_specs=P("rows", None, None, "tm"), check_vma=False
    )
```

```python
import functools
import math

import jax
import jax.numpy as jnp
from jax import lax
from jax.experimental import pallas as pl
from jax.experimental.pallas import tpu as pltpu
from jax.sharding import PartitionSpec as P

F = 64
M = 4
L = 256
T = 2048
S = 512
R = 2048
BLOCK = 32
HALF = 256
TILES = T // L
SCALE = 2.0 * math.pi / L
PEAK = math.sqrt(8.0 / (3.0 * L))
MESH = pl.DeviceIdType.MESH
NT = (((1,), (1,)), ((), ()))


def swap_parts(x):
    rows, cols = x.shape
    return pltpu.roll(x.reshape(rows // 8, 8, cols), 4, 1).reshape(rows, cols)


def split(x):
    high = x.astype(jnp.bfloat16)
    return high, (x - high.astype(jnp.float32)).astype(jnp.bfloat16)


def dot(a, b):
    return jnp.dot(a, b, preferred_element_type=jnp.float32)


def kernel(
    freq_ref, snap_hbm, modes_hbm, off_ref, out_ref,
    snap, modes, d_high, d_low, w_high, w_low, turn, cross, hann, out_turn, out_cross,
    part, landed, total, other,
    snap_sem, own_sem, ag_send, ag_recv, edge_send, edge_recv, rs_send, rs_recv, x_send, x_recv,
):
    tm = lax.axis_index("tm")
    rows = lax.axis_index("rows")
    hi, y, core = tm // 8, (tm // 2) % 4, tm % 2
    lo, z = rows // 8, rows % 8
    way = 1 - 2 * core

    def block_id(h, yy, c):
        return h * 8 + (yy % 4) * 2 + c

    def at(b):
        return modes.at[b // 8, pl.ds(pl.multiple_of((b % 8) * BLOCK, BLOCK), BLOCK), :]

    snap_copy = pltpu.make_async_copy(snap_hbm, snap, snap_sem)
    snap_copy.start()
    own_copy = pltpu.make_async_copy(modes_hbm, at(tm), own_sem)
    own_copy.start()

    mate = block_id(hi, y, 1 - core)
    near = [block_id(hi, y + 1, core), block_id(hi, y + 3, core), block_id(hi, y + 2, core)]
    far = [block_id(1 - hi, y + k, core) for k in (0, 1, 3, 2)]
    below = (tm + 15) % 16
    above = (tm + 1) % 16
    cross_edge = jnp.where(core == 0, below, above)
    z_next = lo * 8 + (z + 8 + way) % 8
    z_prev = lo * 8 + (z + 8 - way) % 8
    x_mate = (1 - lo) * 8 + z

    barrier = pltpu.get_barrier_semaphore()
    for b in [mate, cross_edge] + near + far:
        pl.semaphore_signal(barrier, inc=1, device_id=(b, rows), device_id_type=MESH)
    for r in (z_next, z_prev, x_mate):
        pl.semaphore_signal(barrier, inc=1, device_id=(tm, r), device_id_type=MESH)
    pl.semaphore_wait(barrier, 12)

    sends = []

    def send(src, dst, send_sem, recv_sem, to):
        copy = pltpu.make_async_remote_copy(
            src_ref=src, dst_ref=dst, send_sem=send_sem, recv_sem=recv_sem, device_id=to, device_id_type=MESH
        )
        copy.start()
        sends.append(copy)

    def arrived(dst, recv_sem, to):
        pltpu.make_async_remote_copy(
            src_ref=dst, dst_ref=dst, send_sem=recv_sem, recv_sem=recv_sem, device_id=to, device_id_type=MESH
        ).wait_recv()

    for n, b in enumerate([mate] + near + far):
        send(modes_hbm, at(tm), ag_send.at[n], ag_recv.at[tm], (b, rows))

    def hand_on(n, b):
        arrived(at(b), ag_recv.at[b], (b, rows))
        send(at(b), at(b), ag_send.at[8 + n], ag_recv.at[b], (mate, rows))

    lane = lax.broadcasted_iota(jnp.int32, (8, L), 1)
    upper = lax.broadcasted_iota(jnp.int32, (8, L), 0) < 4

    @pl.loop(0, F, unroll=4)
    def _(f):
        angle = ((freq_ref[f] * lane) & (L - 1)).astype(jnp.float32) * SCALE
        cosine = jnp.cos(angle)
        at_rows = pl.ds(pl.multiple_of((f % 32) * 8, 8), 8)
        turn[f // 32, at_rows, :] = jnp.where(upper, cosine, -cosine)
        cross[f // 32, at_rows, :] = -jnp.sin(angle)

    offsets = off_ref[...]
    upper_out = lax.broadcasted_iota(jnp.int32, (8, S), 0) < 4
    for q in range(4):
        bins = (freq_ref[rows * 4 + q] * jnp.broadcast_to(offsets, (8, S))) & (L - 1)
        angle = bins.astype(jnp.float32) * SCALE
        sine = jnp.sin(angle)
        out_turn[pl.ds(q * 8, 8), :] = jnp.cos(angle)
        out_cross[pl.ds(q * 8, 8), :] = jnp.where(upper_out, -sine, sine)

    for n in range(3):
        hand_on(n, near[n])

    within = offsets & (L - 1)
    tile_of = offsets // L

    @pl.loop(0, L // 32)
    def _(k):
        moment = k * 32 + lax.broadcasted_iota(jnp.int32, (32, S), 0)
        angle = ((moment - within) & (L - 1)).astype(jnp.float32) * SCALE
        hann[pl.ds(pl.multiple_of(k * 32, 32), 32), :] = PEAK * (0.5 - 0.5 * jnp.cos(angle))

    @pl.loop(0, TILES + 1)
    def _(tile):
        @pl.loop(0, L // 32)
        def _(k):
            moment = k * 32 + lax.broadcasted_iota(jnp.int32, (32, S), 0)
            start_tile = jnp.where(moment >= within, tile_of, tile_of + 1)
            values = hann[pl.ds(pl.multiple_of(k * 32, 32), 32), :]
            high, low = split(jnp.where(start_tile == tile, values, 0.0))
            here = pl.ds(pl.multiple_of(tile * L + k * 32, 32), 32)
            w_high[here, :] = high
            w_low[here, :] = low

    own_copy.wait()
    snap_copy.wait()
    arrived(at(mate), ag_recv.at[mate], (mate, rows))
    for k in (1, 3, 2):
        b = block_id(hi, y + k, 1 - core)
        arrived(at(b), ag_recv.at[b], (mate, rows))

    def edge_at(ref, half, tile):
        return ref.at[half, :, pl.ds(tile * L, L)]

    def project(k, tile):
        half = hi if k == 0 else 1 - hi
        p = lax.dot_general(
            modes[half], snap[pl.ds(tile * L, L), :], NT, preferred_element_type=jnp.float32
        )
        high, low = split(turn[half] * p + cross[half] * swap_parts(p))
        d_high[half, :, pl.ds(tile * L, L)] = high
        d_low[half, :, pl.ds(tile * L, L)] = low
        if tile == 0:
            @pl.when(tm > 0)
            def _():
                for n, ref in enumerate((d_high, d_low)):
                    pltpu.make_async_remote_copy(
                        src_ref=edge_at(ref, half, 0), dst_ref=edge_at(ref, half, TILES),
                        send_sem=edge_send.at[half, n], recv_sem=edge_recv.at[half, n],
                        device_id=(below, rows), device_id_type=MESH,
                    ).start()

    def window(k):
        half = hi if k == 0 else 1 - hi

        def sums(first, length, cols):
            at_t = pl.ds(first, length)
            high = d_high[half, :, at_t]
            return (
                dot(high, w_high[at_t, cols])
                + dot(d_low[half, :, at_t], w_high[at_t, cols])
                + dot(high, w_low[at_t, cols])
            )

        for n in range(2):
            cols = pl.ds(n * 256, 256)
            part[k, :, cols] = sums(0, T, cols)

        @pl.when(tm < 15)
        def _():
            for n, ref in enumerate((d_high, d_low)):
                arrived(edge_at(ref, half, TILES), edge_recv.at[half, n], (above, rows))
            part[k] += sums(T, L, pl.ds(0, S))

    def dest(d):
        return pl.ds(pl.multiple_of(((z + 8 + d) % 8) * BLOCK, BLOCK), BLOCK)

    def chain_send(k, n, d, to):
        send(part.at[k, dest(d), :], landed.at[k, n], rs_send.at[k, n], rs_recv.at[k, n], (tm, to))

    def chain_wait(k, n, to):
        arrived(landed.at[k, n], rs_recv.at[k, n], (tm, to))

    def reduce_step(k, step):
        if step == 0:
            chain_send(k, 0, 4 * way, z_next)
            chain_send(k, 4, -3 * way, z_prev)
            return
        chain_wait(k, step - 1, z_prev)
        if step < 4:
            d = (4 - step) * way
            part[k, dest(d), :] += landed[k, step - 1]
            chain_send(k, step, d, z_next)
            chain_wait(k, 3 + step, z_next)
            if step < 3:
                d = (step - 3) * way
                part[k, dest(d), :] += landed[k, 3 + step]
                chain_send(k, 4 + step, d, z_prev)
            return
        total[k] = part[k, dest(0), :] + landed[k, 3] + landed[k, 6]
        half = hi if k == 0 else 1 - hi

        @pl.when(lo != half)
        def _():
            pltpu.make_async_remote_copy(
                src_ref=total.at[k], dst_ref=other, send_sem=x_send, recv_sem=x_recv,
                device_id=(tm, x_mate), device_id_type=MESH,
            ).start()

    for tile in range(TILES):
        project(0, tile)
        if tile == 2:
            for n in range(3):
                hand_on(3 + n, far[n])
        if tile == 5:
            hand_on(6, far[3])
    window(0)
    reduce_step(0, 0)
    for k in (0, 1, 3, 2):
        b = block_id(1 - hi, y + k, 1 - core)
        arrived(at(b), ag_recv.at[b], (mate, rows))
    for tile in range(TILES):
        project(1, tile)
        if tile % 2 == 1:
            reduce_step(0, tile // 2 + 1)
    window(1)
    for step in range(5):
        reduce_step(1, step)

    arrived(other, x_recv, (tm, x_mate))
    mine = jnp.where(lo == hi, 0, 1)
    env = total[mine] + other[...]
    out_ref[...] = out_turn[...] * env + out_cross[...] * swap_parts(env)

    for copy in sends:
        copy.wait_send()

    @pl.when(tm > 0)
    def _():
        for half in range(2):
            for n, ref in enumerate((d_high, d_low)):
                pltpu.make_async_remote_copy(
                    src_ref=edge_at(ref, half, 0), dst_ref=edge_at(ref, half, TILES),
                    send_sem=edge_send.at[half, n], recv_sem=edge_recv.at[half, n],
                    device_id=(below, rows), device_id_type=MESH,
                ).wait_send()

    pltpu.make_async_remote_copy(
        src_ref=total.at[1 - mine], dst_ref=other, send_sem=x_send, recv_sem=x_recv,
        device_id=(tm, x_mate), device_id_type=MESH,
    ).wait_send()


def body(snapshots, spod_modes, freq_index, seg_offsets):
    bf16, f32 = jnp.bfloat16, jnp.float32
    vmem = pltpu.VMEM
    dma = pltpu.SemaphoreType.DMA
    out = pl.pallas_call(
        kernel,
        out_shape=jax.ShapeDtypeStruct((BLOCK, S), f32),
        in_specs=[
            pl.BlockSpec(memory_space=pltpu.SMEM),
            pl.BlockSpec(memory_space=pl.ANY),
            pl.BlockSpec(memory_space=pl.ANY),
            pl.BlockSpec(memory_space=vmem),
        ],
        out_specs=pl.BlockSpec(memory_space=vmem),
        scratch_shapes=[
            vmem((T, R), bf16),
            vmem((2, HALF, R), bf16),
            vmem((2, HALF, T + L), bf16),
            vmem((2, HALF, T + L), bf16),
            vmem((T + L, S), bf16),
            vmem((T + L, S), bf16),
            vmem((2, HALF, L), f32),
            vmem((2, HALF, L), f32),
            vmem((L, S), f32),
            vmem((BLOCK, S), f32),
            vmem((BLOCK, S), f32),
            vmem((2, HALF, S), f32),
            vmem((2, 7, BLOCK, S), f32),
            vmem((2, BLOCK, S), f32),
            vmem((BLOCK, S), f32),
            dma, dma,
            dma((15,)), dma((16,)),
            dma((2, 2)), dma((2, 2)),
            dma((2, 7)), dma((2, 7)),
            dma, dma,
        ],
        compiler_params=pltpu.CompilerParams(
            collective_id=0, has_side_effects=True, vmem_limit_bytes=56 * 1024 * 1024
        ),
        cost_estimate=pl.CostEstimate(flops=8 * 10**9, bytes_accessed=10**7, transcendentals=0),
    )(freq_index, snapshots, spod_modes.reshape(BLOCK, R), seg_offsets.reshape(1, S))
    return out.reshape(F // 16, 2, M, S)


def solution(mesh):
    placed = (P("tm", "rows"), P("tm", None, None, "rows"), P(), P("tm"))
    return jax.shard_map(
        body, mesh=mesh, in_specs=placed, out_specs=P("rows", None, None, "tm"), check_vma=False
    )
```

```python
import functools
import math

import jax
import jax.numpy as jnp
from jax import lax
from jax.experimental import pallas as pl
from jax.experimental.pallas import tpu as pltpu
from jax.sharding import PartitionSpec as P

F = 64
M = 4
L = 256
T = 2048
S = 512
R = 2048
BLOCK = 32
HALF = 256
TILES = T // L
SCALE = 2.0 * math.pi / L
PEAK = math.sqrt(8.0 / (3.0 * L))
MESH = pl.DeviceIdType.MESH
NT = (((1,), (1,)), ((), ()))


def swap_parts(x):
    rows, cols = x.shape
    return pltpu.roll(x.reshape(rows // 8, 8, cols), 4, 1).reshape(rows, cols)


def split(x):
    high = x.astype(jnp.bfloat16)
    return high, (x - high.astype(jnp.float32)).astype(jnp.bfloat16)


def dot(a, b):
    return jnp.dot(a, b, preferred_element_type=jnp.float32)


def kernel(
    freq_ref, snap_hbm, modes_hbm, off_ref, out_ref,
    snap, modes, d_high, d_low, w_high, w_low, turn, cross, hann, out_turn, out_cross,
    part, landed, total, other, raw,
    snap_sem, own_sem, ag_send, ag_recv, edge_send, edge_recv, rs_send, rs_recv, x_send, x_recv,
):
    tm = lax.axis_index("tm")
    rows = lax.axis_index("rows")
    hi, y, core = tm // 8, (tm // 2) % 4, tm % 2
    lo, z = rows // 8, rows % 8
    way = 1 - 2 * core

    def block_id(h, yy, c):
        return h * 8 + (yy % 4) * 2 + c

    def at(b):
        return modes.at[b // 8, pl.ds(pl.multiple_of((b % 8) * BLOCK, BLOCK), BLOCK), :]

    snap_copy = pltpu.make_async_copy(snap_hbm, snap, snap_sem)
    snap_copy.start()
    own_copy = pltpu.make_async_copy(modes_hbm, raw, own_sem)
    own_copy.start()

    mate = block_id(hi, y, 1 - core)
    up, down, opposite = [block_id(hi, y + k, core) for k in (1, 3, 2)]
    peer, peer_up, peer_down, peer_opposite = [block_id(1 - hi, y + k, core) for k in (0, 1, 3, 2)]
    below = (tm + 15) % 16
    above = (tm + 1) % 16
    cross_edge = jnp.where(core == 0, below, above)
    z_next = lo * 8 + (z + 8 + way) % 8
    z_prev = lo * 8 + (z + 8 - way) % 8
    x_mate = (1 - lo) * 8 + z

    barrier = pltpu.get_barrier_semaphore()
    for b in (mate, cross_edge, up, down, peer):
        pl.semaphore_signal(barrier, inc=1, device_id=(b, rows), device_id_type=MESH)
    for r in (z_next, z_prev, x_mate):
        pl.semaphore_signal(barrier, inc=1, device_id=(tm, r), device_id_type=MESH)

    lane = lax.broadcasted_iota(jnp.int32, (8, L), 1)
    upper = lax.broadcasted_iota(jnp.int32, (8, L), 0) < 4

    @pl.loop(0, F, unroll=4)
    def _(f):
        angle = ((freq_ref[f] * lane) & (L - 1)).astype(jnp.float32) * SCALE
        cosine = jnp.cos(angle)
        at_rows = pl.ds(pl.multiple_of((f % 32) * 8, 8), 8)
        turn[f // 32, at_rows, :] = jnp.where(upper, cosine, -cosine)
        cross[f // 32, at_rows, :] = -jnp.sin(angle)

    offsets = off_ref[...]
    upper_out = lax.broadcasted_iota(jnp.int32, (8, S), 0) < 4
    for q in range(4):
        bins = (freq_ref[rows * 4 + q] * jnp.broadcast_to(offsets, (8, S))) & (L - 1)
        angle = bins.astype(jnp.float32) * SCALE
        sine = jnp.sin(angle)
        out_turn[pl.ds(q * 8, 8), :] = jnp.cos(angle)
        out_cross[pl.ds(q * 8, 8), :] = jnp.where(upper_out, -sine, sine)

    within = offsets & (L - 1)
    tile_of = offsets // L

    @pl.loop(0, L // 32)
    def _(k):
        moment = k * 32 + lax.broadcasted_iota(jnp.int32, (32, S), 0)
        angle = ((moment - within) & (L - 1)).astype(jnp.float32) * SCALE
        hann[pl.ds(pl.multiple_of(k * 32, 32), 32), :] = PEAK * (0.5 - 0.5 * jnp.cos(angle))

    @pl.loop(0, TILES + 1)
    def _(tile):
        @pl.loop(0, L // 32)
        def _(k):
            moment = k * 32 + lax.broadcasted_iota(jnp.int32, (32, S), 0)
            start_tile = jnp.where(moment >= within, tile_of, tile_of + 1)
            values = hann[pl.ds(pl.multiple_of(k * 32, 32), 32), :]
            high, low = split(jnp.where(start_tile == tile, values, 0.0))
            here = pl.ds(pl.multiple_of(tile * L + k * 32, 32), 32)
            w_high[here, :] = high
            w_low[here, :] = low

    own_copy.wait()
    own = at(tm)
    for n in range(2):
        pair = [raw[2 * n + q].astype(jnp.float32).reshape(8, R) for q in range(2)]
        own[pl.ds(n * 16, 16), :] = jnp.concatenate(pair, 0).astype(jnp.bfloat16)

    pl.semaphore_wait(barrier, 8)

    sends = []

    def send(src, dst, send_sem, recv_sem, to):
        copy = pltpu.make_async_remote_copy(
            src_ref=src, dst_ref=dst, send_sem=send_sem, recv_sem=recv_sem, device_id=to, device_id_type=MESH
        )
        copy.start()
        sends.append(copy)

    def arrived(dst, recv_sem, to):
        pltpu.make_async_remote_copy(
            src_ref=dst, dst_ref=dst, send_sem=recv_sem, recv_sem=recv_sem, device_id=to, device_id_type=MESH
        ).wait_recv()

    def piece_at(b, piece):
        return modes.at[b // 8, pl.ds(pl.multiple_of((b % 8) * BLOCK + piece * 16, 16), 16), :]

    def send_block(n, b, to):
        send(at(b), at(b), ag_send.at[n], ag_recv.at[b, 0], (to, rows))

    def send_piece(n, b, piece, to):
        here = piece_at(b, piece)
        send(here, here, ag_send.at[n], ag_recv.at[b, piece], (to, rows))

    def block_arrived(b, source):
        arrived(at(b), ag_recv.at[b, 0], (source, rows))

    def piece_arrived(b, piece, source):
        arrived(piece_at(b, piece), ag_recv.at[b, piece], (source, rows))

    send_block(0, tm, peer)
    send_block(1, tm, up)
    send_block(2, tm, down)
    send_block(3, tm, mate)
    block_arrived(up, up)
    send_piece(4, up, 0, down)
    block_arrived(down, down)
    send_piece(5, down, 1, up)
    send_block(6, up, mate)
    send_block(7, down, mate)
    block_arrived(peer, peer)
    send_block(8, peer, up)
    send_block(9, peer, down)
    send_block(10, peer, mate)
    piece_arrived(opposite, 0, up)
    send_piece(11, opposite, 0, peer)
    piece_arrived(opposite, 1, down)
    send_piece(12, opposite, 1, peer)
    send_block(13, opposite, mate)

    snap_copy.wait()
    for k in (0, 1, 3, 2):
        block_arrived(block_id(hi, y + k, 1 - core), mate)

    def edge_at(ref, half, tile):
        return ref.at[half, :, pl.ds(tile * L, L)]

    def project(k, tile):
        half = hi if k == 0 else 1 - hi
        p = lax.dot_general(
            modes[half], snap[pl.ds(tile * L, L), :], NT, preferred_element_type=jnp.float32
        )
        high, low = split(turn[half] * p + cross[half] * swap_parts(p))
        d_high[half, :, pl.ds(tile * L, L)] = high
        d_low[half, :, pl.ds(tile * L, L)] = low
        if tile == 0:
            @pl.when(tm > 0)
            def _():
                for n, ref in enumerate((d_high, d_low)):
                    pltpu.make_async_remote_copy(
                        src_ref=edge_at(ref, half, 0), dst_ref=edge_at(ref, half, TILES),
                        send_sem=edge_send.at[half, n], recv_sem=edge_recv.at[half, n],
                        device_id=(below, rows), device_id_type=MESH,
                    ).start()

    def sums(half, first, length, cols):
        at_t = pl.ds(first, length)
        high = d_high[half, :, at_t]
        return (
            dot(high, w_high[at_t, cols])
            + dot(d_low[half, :, at_t], w_high[at_t, cols])
            + dot(high, w_low[at_t, cols])
        )

    def half_of(k):
        return hi if k == 0 else 1 - hi

    def columns(n):
        return pl.ds(n * 256, 256)

    def window(k, n):
        part[k, :, columns(n)] = sums(half_of(k), 0, T, columns(n))

    def edge_arrived(k):
        @pl.when(tm < 15)
        def _():
            for n, ref in enumerate((d_high, d_low)):
                arrived(edge_at(ref, half_of(k), TILES), edge_recv.at[half_of(k), n], (above, rows))

    def window_edge(k, n):
        @pl.when(tm < 15)
        def _():
            part[k, :, columns(n)] += sums(half_of(k), T, L, columns(n))

    def dest(d):
        return pl.ds(pl.multiple_of(((z + 8 + d) % 8) * BLOCK, BLOCK), BLOCK)

    def chain_send(k, n, i, d, to):
        send(
            part.at[k, dest(d), columns(n)], landed.at[k, n, i], rs_send.at[k, n, i], rs_recv.at[k, n, i], (tm, to)
        )

    def chain_add(k, n, i, d, source):
        arrived(landed.at[k, n, i], rs_recv.at[k, n, i], (tm, source))
        part[k, dest(d), columns(n)] += landed[k, n, i]

    def reduce_step(k, n, step):
        if step > 0:
            chain_add(k, n, step - 1, (4 - step) * way, z_prev)
        if step < 4:
            chain_send(k, n, step, (4 - step) * way, z_next)
            if step > 0:
                chain_add(k, n, 3 + step, (step - 3) * way, z_next)
            if step < 3:
                chain_send(k, n, 4 + step, (step - 3) * way, z_prev)
            return
        total[k, n] = part[k, dest(0), columns(n)]

        @pl.when(lo != half_of(k))
        def _():
            pltpu.make_async_remote_copy(
                src_ref=total.at[k, n], dst_ref=other.at[n], send_sem=x_send.at[n], recv_sem=x_recv.at[n],
                device_id=(tm, x_mate), device_id_type=MESH,
            ).start()

    for tile in range(TILES):
        project(0, tile)
        if tile == 4:
            for n, b in enumerate((peer_up, peer_down)):
                block_arrived(b, (up, down)[n])
                send_block(14 + n, b, mate)
    for piece in range(2):
        piece_arrived(peer_opposite, piece, peer)
    send_block(16, peer_opposite, mate)
    for n in range(2):
        window(0, n)
    for k in (0, 1, 3, 2):
        block_arrived(block_id(1 - hi, y + k, 1 - core), mate)
    project(1, 0)
    project(1, 1)
    edge_arrived(0)
    for n in range(2):
        window_edge(0, n)
        reduce_step(0, n, 0)
    for tile in range(2, TILES):
        project(1, tile)
    for n in range(2):
        reduce_step(0, n, 1)
    edge_arrived(1)
    for n in range(2):
        window(1, n)
        window_edge(1, n)
        reduce_step(1, n, 0)
        for m in range(2):
            reduce_step(0, m, 2 + n)
    for n in range(2):
        reduce_step(0, n, 4)
    for step in range(1, 5):
        for n in range(2):
            reduce_step(1, n, step)

    mine = jnp.where(lo == hi, 0, 1)
    for n in range(2):
        arrived(other.at[n], x_recv.at[n], (tm, x_mate))
        env = total[mine, n] + other[n]
        result = out_turn[:, columns(n)] * env + out_cross[:, columns(n)] * swap_parts(env)
        for q in range(4):
            for p in range(2):
                out_ref[q, p, :, columns(n)] = result[q * 8 + p * 4:q * 8 + p * 4 + 4]

    for copy in sends:
        copy.wait_send()

    @pl.when(tm > 0)
    def _():
        for half in range(2):
            for n, ref in enumerate((d_high, d_low)):
                pltpu.make_async_remote_copy(
                    src_ref=edge_at(ref, half, 0), dst_ref=edge_at(ref, half, TILES),
                    send_sem=edge_send.at[half, n], recv_sem=edge_recv.at[half, n],
                    device_id=(below, rows), device_id_type=MESH,
                ).wait_send()

    for n in range(2):
        pltpu.make_async_remote_copy(
            src_ref=total.at[1 - mine, n], dst_ref=other.at[n], send_sem=x_send.at[n], recv_sem=x_recv.at[n],
            device_id=(tm, x_mate), device_id_type=MESH,
        ).wait_send()


def body(snapshots, spod_modes, freq_index, seg_offsets):
    bf16, f32 = jnp.bfloat16, jnp.float32
    vmem = pltpu.VMEM
    dma = pltpu.SemaphoreType.DMA
    return pl.pallas_call(
        kernel,
        out_shape=jax.ShapeDtypeStruct((F // 16, 2, M, S), f32),
        in_specs=[
            pl.BlockSpec(memory_space=pltpu.SMEM),
            pl.BlockSpec(memory_space=pl.ANY),
            pl.BlockSpec(memory_space=pl.ANY),
            pl.BlockSpec(memory_space=vmem),
        ],
        out_specs=pl.BlockSpec(memory_space=vmem),
        scratch_shapes=[
            vmem((T, R), bf16),
            vmem((2, HALF, R), bf16),
            vmem((2, HALF, T + L), bf16),
            vmem((2, HALF, T + L), bf16),
            vmem((T + L, S), bf16),
            vmem((T + L, S), bf16),
            vmem((2, HALF, L), f32),
            vmem((2, HALF, L), f32),
            vmem((L, S), f32),
            vmem((BLOCK, S), f32),
            vmem((BLOCK, S), f32),
            vmem((2, HALF, S), f32),
            vmem((2, 2, 7, BLOCK, 256), f32),
            vmem((2, 2, BLOCK, 256), f32),
            vmem((2, BLOCK, 256), f32),
            vmem((F // 16, 2, M, R), bf16),
            dma, dma,
            dma((17,)), dma((16, 2)),
            dma((2, 2)), dma((2, 2)),
            dma((2, 2, 7)), dma((2, 2, 7)),
            dma((2,)), dma((2,)),
        ],
        compiler_params=pltpu.CompilerParams(
            collective_id=0, has_side_effects=True, vmem_limit_bytes=56 * 1024 * 1024
        ),
        cost_estimate=pl.CostEstimate(flops=8 * 10**9, bytes_accessed=10**7, transcendentals=0),
    )(freq_index, snapshots, spod_modes, seg_offsets.reshape(1, S))


def solution(mesh):
    placed = (P("tm", "rows"), P("tm", None, None, "rows"), P(), P("tm"))
    return jax.shard_map(
        body, mesh=mesh, in_specs=placed, out_specs=P("rows", None, None, "tm"), check_vma=False
    )
```

```python
import functools
import math

import jax
import jax.numpy as jnp
from jax import lax
from jax.experimental import pallas as pl
from jax.experimental.pallas import tpu as pltpu
from jax.sharding import PartitionSpec as P

F = 64
M = 4
L = 256
T = 2048
S = 512
R = 2048
BLOCK = 32
HALF = 256
TILES = T // L
SCALE = 2.0 * math.pi / L
PEAK = math.sqrt(8.0 / (3.0 * L))
CODES = 32767.0
MESH = pl.DeviceIdType.MESH
NT = (((1,), (1,)), ((), ()))


def swap_parts(x):
    rows, cols = x.shape
    return pltpu.roll(x.reshape(rows // 8, 8, cols), 4, 1).reshape(rows, cols)


def split(x):
    high = x.astype(jnp.bfloat16)
    return high, (x - high.astype(jnp.float32)).astype(jnp.bfloat16)


def dot(a, b):
    return jnp.dot(a, b, preferred_element_type=jnp.float32)


def kernel(
    freq_ref, snap_hbm, modes_hbm, off_ref, out_ref,
    snap, modes, d_high, d_low, w_high, w_low, turn, cross, hann, out_turn, out_cross,
    part, codes, landed, raw, total,
    snap_sem, own_sem, ag_send, ag_recv, edge_send, edge_recv, rs_send, rs_recv,
):
    tm = lax.axis_index("tm")
    rows = lax.axis_index("rows")
    hi, y, core = tm // 8, (tm // 2) % 4, tm % 2
    lo, z = rows // 8, rows % 8

    def block_id(h, yy, c):
        return h * 8 + (yy % 4) * 2 + c

    def at(b):
        return modes.at[b // 8, pl.ds(pl.multiple_of((b % 8) * BLOCK, BLOCK), BLOCK), :]

    snap_copy = pltpu.make_async_copy(snap_hbm, snap, snap_sem)
    snap_copy.start()
    own_copy = pltpu.make_async_copy(modes_hbm, raw, own_sem)
    own_copy.start()

    mate = block_id(hi, y, 1 - core)
    up, down, opposite = [block_id(hi, y + k, core) for k in (1, 3, 2)]
    peer, peer_up, peer_down, peer_opposite = [block_id(1 - hi, y + k, core) for k in (0, 1, 3, 2)]
    below = (tm + 15) % 16
    above = (tm + 1) % 16
    cross_edge = jnp.where(core == 0, below, above)

    barrier = pltpu.get_barrier_semaphore()
    for b in (mate, cross_edge, up, down, opposite, peer):
        pl.semaphore_signal(barrier, inc=1, device_id=(b, rows), device_id_type=MESH)
    for d in range(1, 16):
        pl.semaphore_signal(barrier, inc=1, device_id=(tm, (rows + d) % 16), device_id_type=MESH)

    lane = lax.broadcasted_iota(jnp.int32, (8, L), 1)
    upper = lax.broadcasted_iota(jnp.int32, (8, L), 0) < 4

    @pl.loop(0, F, unroll=4)
    def _(f):
        angle = ((freq_ref[f] * lane) & (L - 1)).astype(jnp.float32) * SCALE
        cosine = jnp.cos(angle)
        at_rows = pl.ds(pl.multiple_of((f % 32) * 8, 8), 8)
        turn[f // 32, at_rows, :] = jnp.where(upper, cosine, -cosine)
        cross[f // 32, at_rows, :] = -jnp.sin(angle)

    offsets = off_ref[...]
    upper_out = lax.broadcasted_iota(jnp.int32, (8, S), 0) < 4
    for q in range(4):
        bins = (freq_ref[rows * 4 + q] * jnp.broadcast_to(offsets, (8, S))) & (L - 1)
        angle = bins.astype(jnp.float32) * SCALE
        sine = jnp.sin(angle)
        out_turn[pl.ds(q * 8, 8), :] = jnp.cos(angle)
        out_cross[pl.ds(q * 8, 8), :] = jnp.where(upper_out, -sine, sine)

    within = offsets & (L - 1)
    tile_of = offsets // L

    @pl.loop(0, L // 32)
    def _(k):
        moment = k * 32 + lax.broadcasted_iota(jnp.int32, (32, S), 0)
        angle = ((moment - within) & (L - 1)).astype(jnp.float32) * SCALE
        hann[pl.ds(pl.multiple_of(k * 32, 32), 32), :] = PEAK * (0.5 - 0.5 * jnp.cos(angle))

    @pl.loop(0, TILES + 1)
    def _(tile):
        @pl.loop(0, L // 32)
        def _(k):
            moment = k * 32 + lax.broadcasted_iota(jnp.int32, (32, S), 0)
            start_tile = jnp.where(moment >= within, tile_of, tile_of + 1)
            values = hann[pl.ds(pl.multiple_of(k * 32, 32), 32), :]
            high, low = split(jnp.where(start_tile == tile, values, 0.0))
            here = pl.ds(pl.multiple_of(tile * L + k * 32, 32), 32)
            w_high[here, :] = high
            w_low[here, :] = low

    own_copy.wait()
    own = at(tm)
    for n in range(2):
        pair = [raw[2 * n + q].astype(jnp.float32).reshape(8, R) for q in range(2)]
        own[pl.ds(n * 16, 16), :] = jnp.concatenate(pair, 0).astype(jnp.bfloat16)

    pl.semaphore_wait(barrier, 21)

    sends = []

    def send(src, dst, send_sem, recv_sem, to):
        copy = pltpu.make_async_remote_copy(
            src_ref=src, dst_ref=dst, send_sem=send_sem, recv_sem=recv_sem, device_id=to, device_id_type=MESH
        )
        copy.start()
        sends.append(copy)

    def arrived(dst, recv_sem, to):
        pltpu.make_async_remote_copy(
            src_ref=dst, dst_ref=dst, send_sem=recv_sem, recv_sem=recv_sem, device_id=to, device_id_type=MESH
        ).wait_recv()

    def send_block(n, b, to):
        send(at(b), at(b), ag_send.at[n], ag_recv.at[b], (to, rows))

    def block_arrived(b, source):
        arrived(at(b), ag_recv.at[b], (source, rows))

    send_block(0, tm, opposite)
    send_block(1, tm, peer)
    send_block(2, tm, up)
    send_block(3, tm, down)
    send_block(4, tm, mate)
    block_arrived(opposite, opposite)
    send_block(5, opposite, peer)
    block_arrived(peer, peer)
    send_block(6, peer, up)
    send_block(7, peer, down)
    send_block(8, opposite, mate)
    block_arrived(up, up)
    send_block(9, up, mate)
    block_arrived(down, down)
    send_block(10, down, mate)
    send_block(11, peer, mate)

    snap_copy.wait()
    for k in (0, 2, 1, 3):
        block_arrived(block_id(hi, y + k, 1 - core), mate)

    def edge_at(ref, half, tile):
        return ref.at[half, :, pl.ds(tile * L, L)]

    def project(k, tile):
        half = hi if k == 0 else 1 - hi
        p = lax.dot_general(
            modes[half], snap[pl.ds(tile * L, L), :], NT, preferred_element_type=jnp.float32
        )
        high, low = split(turn[half] * p + cross[half] * swap_parts(p))
        d_high[half, :, pl.ds(tile * L, L)] = high
        d_low[half, :, pl.ds(tile * L, L)] = low
        if tile == 0:
            @pl.when(tm > 0)
            def _():
                for n, ref in enumerate((d_high, d_low)):
                    pltpu.make_async_remote_copy(
                        src_ref=edge_at(ref, half, 0), dst_ref=edge_at(ref, half, TILES),
                        send_sem=edge_send.at[half, n], recv_sem=edge_recv.at[half, n],
                        device_id=(below, rows), device_id_type=MESH,
                    ).start()

    def sums(half, first, length, cols):
        at_t = pl.ds(first, length)
        high = d_high[half, :, at_t]
        return (
            dot(high, w_high[at_t, cols])
            + dot(d_low[half, :, at_t], w_high[at_t, cols])
            + dot(high, w_low[at_t, cols])
        )

    def half_of(k):
        return hi if k == 0 else 1 - hi

    def columns(n):
        return pl.ds(n * 256, 256)

    def window(k, n):
        part[k, :, columns(n)] = sums(half_of(k), 0, T, columns(n))

    def edge_arrived(k):
        @pl.when(tm < 15)
        def _():
            for n, ref in enumerate((d_high, d_low)):
                arrived(edge_at(ref, half_of(k), TILES), edge_recv.at[half_of(k), n], (above, rows))

    def window_edge(k, n):
        @pl.when(tm < 15)
        def _():
            part[k, :, columns(n)] += sums(half_of(k), T, L, columns(n))

    def block_rows(d):
        return ((z + d) % 8) * BLOCK

    def encode(k, d):
        first = block_rows(d)
        powers = []
        for pair in range(2):
            rounded = []
            for q in (2 * pair, 2 * pair + 1):
                x = part[k, pl.ds(pl.multiple_of(first + q * 8, 8), 8), :]
                largest = jnp.max(jnp.abs(x), axis=(0, 1), keepdims=True)
                largest = jnp.broadcast_to(jnp.maximum(largest, 1e-30), (8, 128))
                power = jnp.ceil(16.0 * jnp.log2(largest)) + 1.0
                inverse = CODES / jnp.exp2(power * 0.0625)
                rounded.append(jnp.round(x * jnp.concatenate([inverse] * 4, 1)).astype(jnp.int32))
                powers.append(power[:4])
            pair_codes = jnp.concatenate(rounded, 0).astype(jnp.int16)
            for g in range(4):
                codes[k, d, pl.ds(g * BLOCK + pair * 16, 16), :] = pair_codes[:, g * 128:(g + 1) * 128]
        codes[k, d, pl.ds(4 * BLOCK, 16), :] = jnp.concatenate(powers, 0).astype(jnp.int32).astype(jnp.int16)

    def code_copy(k, d):
        half = half_of(k)
        slot = jnp.where(lo == half, 0, 8) + d
        return pltpu.make_async_remote_copy(
            src_ref=codes.at[k, d], dst_ref=landed.at[slot], send_sem=rs_send.at[k, d], recv_sem=rs_recv.at[slot],
            device_id=(tm, half * 8 + (z + d) % 8), device_id_type=MESH,
        )

    def send_codes(k):
        for d in (4, 3, 5, 2, 6, 1, 7):
            encode(k, d)
            code_copy(k, d).start()

        @pl.when(lo != half_of(k))
        def _():
            encode(k, 0)
            code_copy(k, 0).start()

    for tile in range(TILES):
        project(0, tile)
    for n, b in enumerate((peer_up, peer_down)):
        block_arrived(b, (up, down)[n])
        send_block(12 + n, b, mate)
    window(0, 0)
    block_arrived(peer_opposite, peer)
    send_block(14, peer_opposite, mate)
    window(0, 1)
    for k in (0, 1, 3, 2):
        block_arrived(block_id(1 - hi, y + k, 1 - core), mate)
    project(1, 0)
    project(1, 1)
    edge_arrived(0)
    for n in range(2):
        window_edge(0, n)
    send_codes(0)
    for tile in range(2, TILES):
        project(1, tile)
    for n in range(2):
        window(1, n)
    edge_arrived(1)
    for n in range(2):
        window_edge(1, n)
    send_codes(1)

    mine = jnp.where(lo == hi, 0, 1)
    total[...] = part[mine, pl.ds(pl.multiple_of(block_rows(0), BLOCK), BLOCK), :]
    for slot in (9, 15, 1, 7, 8, 10, 14, 2, 6, 11, 13, 3, 5, 12, 4):
        pltpu.make_async_remote_copy(
            src_ref=landed.at[slot], dst_ref=landed.at[slot], send_sem=rs_recv.at[slot], recv_sem=rs_recv.at[slot],
            device_id=(tm, (rows + 1) % 16), device_id_type=MESH,
        ).wait_recv()
        power = landed[slot, pl.ds(4 * BLOCK, 16), :].astype(jnp.int32).astype(jnp.float32)
        scale = jnp.exp2(power * 0.0625) * (1.0 / CODES)
        scale = jnp.concatenate([jnp.broadcast_to(scale[4 * q:4 * q + 1], (8, 128)) for q in range(4)], 0)
        for g in range(4):
            values = landed[slot, pl.ds(g * BLOCK, BLOCK), :].astype(jnp.int32).astype(jnp.float32)
            total[:, pl.ds(g * 128, 128)] += values * scale
    env = total[...]
    result = out_turn[...] * env + out_cross[...] * swap_parts(env)
    for q in range(4):
        for p in range(2):
            out_ref[q, p] = result[q * 8 + p * 4:q * 8 + p * 4 + 4]

    for k in range(2):
        for d in range(1, 8):
            code_copy(k, d).wait_send()
    code_copy_left = pltpu.make_async_remote_copy(
        src_ref=codes.at[1 - mine, 0], dst_ref=landed.at[8], send_sem=rs_send.at[1 - mine, 0], recv_sem=rs_recv.at[8],
        device_id=(tm, (1 - lo) * 8 + z), device_id_type=MESH,
    )
    code_copy_left.wait_send()
    for copy in sends:
        copy.wait_send()

    @pl.when(tm > 0)
    def _():
        for half in range(2):
            for n, ref in enumerate((d_high, d_low)):
                pltpu.make_async_remote_copy(
                    src_ref=edge_at(ref, half, 0), dst_ref=edge_at(ref, half, TILES),
                    send_sem=edge_send.at[half, n], recv_sem=edge_recv.at[half, n],
                    device_id=(below, rows), device_id_type=MESH,
                ).wait_send()


def body(snapshots, spod_modes, freq_index, seg_offsets):
    bf16, f32 = jnp.bfloat16, jnp.float32
    vmem = pltpu.VMEM
    dma = pltpu.SemaphoreType.DMA
    return pl.pallas_call(
        kernel,
        out_shape=jax.ShapeDtypeStruct((F // 16, 2, M, S), f32),
        in_specs=[
            pl.BlockSpec(memory_space=pltpu.SMEM),
            pl.BlockSpec(memory_space=pl.ANY),
            pl.BlockSpec(memory_space=pl.ANY),
            pl.BlockSpec(memory_space=vmem),
        ],
        out_specs=pl.BlockSpec(memory_space=vmem),
        scratch_shapes=[
            vmem((T, R), bf16),
            vmem((2, HALF, R), bf16),
            vmem((2, HALF, T + L), bf16),
            vmem((2, HALF, T + L), bf16),
            vmem((T + L, S), bf16),
            vmem((T + L, S), bf16),
            vmem((2, HALF, L), f32),
            vmem((2, HALF, L), f32),
            vmem((L, S), f32),
            vmem((BLOCK, S), f32),
            vmem((BLOCK, S), f32),
            vmem((2, HALF, S), f32),
            vmem((2, 8, 4 * BLOCK + 16, 128), jnp.int16),
            vmem((16, 4 * BLOCK + 16, 128), jnp.int16),
            vmem((F // 16, 2, M, R), bf16),
            vmem((BLOCK, S), f32),
            dma, dma,
            dma((15,)), dma((16,)),
            dma((2, 2)), dma((2, 2)),
            dma((2, 8)), dma((16,)),
        ],
        compiler_params=pltpu.CompilerParams(
            collective_id=0, has_side_effects=True, vmem_limit_bytes=56 * 1024 * 1024
        ),
        cost_estimate=pl.CostEstimate(flops=8 * 10**9, bytes_accessed=10**7, transcendentals=0),
    )(freq_index, snapshots, spod_modes, seg_offsets.reshape(1, S))


def solution(mesh):
    placed = (P("tm", "rows"), P("tm", None, None, "rows"), P(), P("tm"))
    return jax.shard_map(
        body, mesh=mesh, in_specs=placed, out_specs=P("rows", None, None, "tm"), check_vma=False
    )
```

```python
import functools
import math

import jax
import jax.numpy as jnp
from jax import lax
from jax.experimental import pallas as pl
from jax.experimental.pallas import tpu as pltpu
from jax.sharding import PartitionSpec as P

F = 64
M = 4
L = 256
T = 2048
S = 512
R = 2048
BLOCK = 32
HALF = 256
TILES = T // L
SCALE = 2.0 * math.pi / L
PEAK = math.sqrt(8.0 / (3.0 * L))
CODES = 32767.0
MESH = pl.DeviceIdType.MESH
NT = (((1,), (1,)), ((), ()))


def swap_parts(x):
    rows, cols = x.shape
    return pltpu.roll(x.reshape(rows // 8, 8, cols), 4, 1).reshape(rows, cols)


def split(x):
    high = x.astype(jnp.bfloat16)
    return high, (x - high.astype(jnp.float32)).astype(jnp.bfloat16)


def dot(a, b):
    return jnp.dot(a, b, preferred_element_type=jnp.float32)


def to_codes(x):
    return jnp.round(x).astype(jnp.int32).astype(jnp.int16)


def from_codes(codes):
    return codes.astype(jnp.int32).astype(jnp.float32)


def power_above(largest):
    return jnp.ceil(16.0 * jnp.log2(jnp.maximum(largest, 1e-30))) + 1.0


def kernel(
    freq_ref, snap_hbm, modes_hbm, off_ref, out_ref,
    snap, modes, d_high, d_low, w_high, w_low, turn, cross, hann, out_turn, out_cross,
    part, codes, landed, raw, total, edge_out, edge_in,
    snap_sem, own_sem, ag_send, ag_recv, edge_send, edge_recv, rs_send, rs_recv,
):
    tm = lax.axis_index("tm")
    rows = lax.axis_index("rows")
    hi, y, core = tm // 8, (tm // 2) % 4, tm % 2
    lo, z = rows // 8, rows % 8

    def block_id(h, yy, c):
        return h * 8 + (yy % 4) * 2 + c

    def at(b):
        return modes.at[b // 8, pl.ds(pl.multiple_of((b % 8) * BLOCK, BLOCK), BLOCK), :]

    snap_copy = pltpu.make_async_copy(snap_hbm, snap, snap_sem)
    snap_copy.start()
    own_copy = pltpu.make_async_copy(modes_hbm, raw, own_sem)
    own_copy.start()

    mate = block_id(hi, y, 1 - core)
    up, down, opposite = [block_id(hi, y + k, core) for k in (1, 3, 2)]
    peer, peer_up, peer_down, peer_opposite = [block_id(1 - hi, y + k, core) for k in (0, 1, 3, 2)]
    below = (tm + 15) % 16
    above = (tm + 1) % 16
    cross_edge = jnp.where(core == 0, below, above)

    barrier = pltpu.get_barrier_semaphore()
    for b in (mate, cross_edge, up, down, opposite, peer):
        pl.semaphore_signal(barrier, inc=1, device_id=(b, rows), device_id_type=MESH)
    for d in range(1, 16):
        pl.semaphore_signal(barrier, inc=1, device_id=(tm, (rows + d) % 16), device_id_type=MESH)

    lane = lax.broadcasted_iota(jnp.int32, (8, L), 1)
    upper = lax.broadcasted_iota(jnp.int32, (8, L), 0) < 4

    @pl.loop(0, F, unroll=4)
    def _(f):
        angle = ((freq_ref[f] * lane) & (L - 1)).astype(jnp.float32) * SCALE
        cosine = jnp.cos(angle)
        at_rows = pl.ds(pl.multiple_of((f % 32) * 8, 8), 8)
        turn[f // 32, at_rows, :] = jnp.where(upper, cosine, -cosine)
        cross[f // 32, at_rows, :] = -jnp.sin(angle)

    offsets = off_ref[...]
    upper_out = lax.broadcasted_iota(jnp.int32, (8, S), 0) < 4
    for q in range(4):
        bins = (freq_ref[rows * 4 + q] * jnp.broadcast_to(offsets, (8, S))) & (L - 1)
        angle = bins.astype(jnp.float32) * SCALE
        sine = jnp.sin(angle)
        out_turn[pl.ds(q * 8, 8), :] = jnp.cos(angle)
        out_cross[pl.ds(q * 8, 8), :] = jnp.where(upper_out, -sine, sine)

    within = offsets & (L - 1)
    tile_of = offsets // L

    @pl.loop(0, L // 32)
    def _(k):
        moment = k * 32 + lax.broadcasted_iota(jnp.int32, (32, S), 0)
        angle = ((moment - within) & (L - 1)).astype(jnp.float32) * SCALE
        hann[pl.ds(pl.multiple_of(k * 32, 32), 32), :] = PEAK * (0.5 - 0.5 * jnp.cos(angle))

    @pl.loop(0, TILES + 1)
    def _(tile):
        @pl.loop(0, L // 32)
        def _(k):
            moment = k * 32 + lax.broadcasted_iota(jnp.int32, (32, S), 0)
            start_tile = jnp.where(moment >= within, tile_of, tile_of + 1)
            values = hann[pl.ds(pl.multiple_of(k * 32, 32), 32), :]
            high, low = split(jnp.where(start_tile == tile, values, 0.0))
            here = pl.ds(pl.multiple_of(tile * L + k * 32, 32), 32)
            w_high[here, :] = high
            w_low[here, :] = low

    own_copy.wait()
    own = at(tm)
    for n in range(2):
        pair = [raw[2 * n + q].astype(jnp.float32).reshape(8, R) for q in range(2)]
        own[pl.ds(n * 16, 16), :] = jnp.concatenate(pair, 0).astype(jnp.bfloat16)

    pl.semaphore_wait(barrier, 21)

    sends = []

    def send(src, dst, send_sem, recv_sem, to):
        copy = pltpu.make_async_remote_copy(
            src_ref=src, dst_ref=dst, send_sem=send_sem, recv_sem=recv_sem, device_id=to, device_id_type=MESH
        )
        copy.start()
        sends.append(copy)

    def arrived(dst, recv_sem, to):
        pltpu.make_async_remote_copy(
            src_ref=dst, dst_ref=dst, send_sem=recv_sem, recv_sem=recv_sem, device_id=to, device_id_type=MESH
        ).wait_recv()

    def send_block(n, b, to):
        send(at(b), at(b), ag_send.at[n], ag_recv.at[b], (to, rows))

    def block_arrived(b, source):
        arrived(at(b), ag_recv.at[b], (source, rows))

    send_block(0, tm, opposite)
    send_block(1, tm, peer)
    send_block(2, tm, up)
    send_block(3, tm, down)
    send_block(4, tm, mate)
    block_arrived(opposite, opposite)
    send_block(5, opposite, peer)
    block_arrived(peer, peer)
    send_block(6, peer, up)
    send_block(7, peer, down)
    send_block(8, opposite, mate)
    block_arrived(up, up)
    send_block(9, up, mate)
    block_arrived(down, down)
    send_block(10, down, mate)
    send_block(11, peer, mate)

    snap_copy.wait()
    for k in (0, 2, 1, 3):
        block_arrived(block_id(hi, y + k, 1 - core), mate)

    def edge_copy(half):
        return pltpu.make_async_remote_copy(
            src_ref=edge_out.at[half], dst_ref=edge_in.at[half],
            send_sem=edge_send.at[half], recv_sem=edge_recv.at[half],
            device_id=(below, rows), device_id_type=MESH,
        )

    def half_of(k):
        return hi if k == 0 else 1 - hi

    def to_rows(x):
        return jnp.broadcast_to(x[:, None, :], (32, 8, 128)).reshape(HALF, 128)

    def project(k, tile):
        half = half_of(k)
        p = lax.dot_general(
            modes[half], snap[pl.ds(tile * L, L), :], NT, preferred_element_type=jnp.float32
        )
        d = turn[half] * p + cross[half] * swap_parts(p)
        if tile == 0:
            largest = jnp.max(jnp.abs(d), axis=1, keepdims=True)
            largest = jnp.max(jnp.broadcast_to(largest, (HALF, 128)).reshape(32, 8, 128), axis=1)
            power = power_above(largest)
            inverse = to_rows(CODES / jnp.exp2(power * 0.0625))
            edge_out[half, pl.ds(HALF, 32), :] = to_codes(jnp.concatenate([power] * 2, 1))
            edge_out[half, pl.ds(0, HALF), :] = to_codes(d * jnp.concatenate([inverse] * 2, 1))

            @pl.when(tm > 0)
            def _():
                edge_copy(half).start()

        high, low = split(d)
        d_high[half, :, pl.ds(tile * L, L)] = high
        d_low[half, :, pl.ds(tile * L, L)] = low

    def sums(half, first, length, cols):
        at_t = pl.ds(first, length)
        high = d_high[half, :, at_t]
        return (
            dot(high, w_high[at_t, cols])
            + dot(d_low[half, :, at_t], w_high[at_t, cols])
            + dot(high, w_low[at_t, cols])
        )

    def columns(n):
        return pl.ds(n * 256, 256)

    def window(k, n):
        part[k, :, columns(n)] = sums(half_of(k), 0, T, columns(n))

    def edge_arrived(k):
        half = half_of(k)

        @pl.when(tm < 15)
        def _():
            arrived(edge_in.at[half], edge_recv.at[half], (above, rows))
            power = from_codes(edge_in[half, pl.ds(HALF, 32), pl.ds(0, 128)])
            scale = to_rows(jnp.exp2(power * 0.0625) * (1.0 / CODES))
            values = from_codes(edge_in[half, pl.ds(0, HALF), :])
            high, low = split(values * jnp.concatenate([scale] * 2, 1))
            d_high[half, :, pl.ds(T, L)] = high
            d_low[half, :, pl.ds(T, L)] = low

    def window_edge(k, n):
        @pl.when(tm < 15)
        def _():
            part[k, :, columns(n)] += sums(half_of(k), T, L, columns(n))

    def block_rows(d):
        return ((z + d) % 8) * BLOCK

    def encode(k, d):
        first = block_rows(d)
        powers = []
        for pair in range(2):
            rounded = []
            for q in (2 * pair, 2 * pair + 1):
                x = part[k, pl.ds(pl.multiple_of(first + q * 8, 8), 8), :]
                largest = jnp.max(jnp.abs(x), axis=(0, 1), keepdims=True)
                power = power_above(jnp.broadcast_to(largest, (8, 128)))
                inverse = CODES / jnp.exp2(power * 0.0625)
                rounded.append(jnp.round(x * jnp.concatenate([inverse] * 4, 1)).astype(jnp.int32))
                powers.append(power[:4])
            pair_codes = jnp.concatenate(rounded, 0).astype(jnp.int16)
            for g in range(4):
                codes[k, d, pl.ds(g * BLOCK + pair * 16, 16), :] = pair_codes[:, g * 128:(g + 1) * 128]
        codes[k, d, pl.ds(4 * BLOCK, 16), :] = jnp.concatenate(powers, 0).astype(jnp.int32).astype(jnp.int16)

    def code_copy(k, d):
        half = half_of(k)
        slot = jnp.where(lo == half, 0, 8) + d
        return pltpu.make_async_remote_copy(
            src_ref=codes.at[k, d], dst_ref=landed.at[slot], send_sem=rs_send.at[k, d], recv_sem=rs_recv.at[slot],
            device_id=(tm, half * 8 + (z + d) % 8), device_id_type=MESH,
        )

    def send_codes(k):
        for d in (4, 3, 5, 2, 6, 1, 7):
            encode(k, d)
            code_copy(k, d).start()

        @pl.when(lo != half_of(k))
        def _():
            encode(k, 0)
            code_copy(k, 0).start()

    for tile in range(TILES):
        project(0, tile)
    for n, b in enumerate((peer_up, peer_down)):
        block_arrived(b, (up, down)[n])
        send_block(12 + n, b, mate)
    window(0, 0)
    block_arrived(peer_opposite, peer)
    send_block(14, peer_opposite, mate)
    window(0, 1)
    for k in (0, 1, 3, 2):
        block_arrived(block_id(1 - hi, y + k, 1 - core), mate)
    project(1, 0)
    project(1, 1)

    def finish_first():
        edge_arrived(0)
        for n in range(2):
            window_edge(0, n)
        send_codes(0)

    pl.when(tm != 7)(finish_first)
    for tile in range(2, TILES):
        project(1, tile)
    pl.when(tm == 7)(finish_first)
    for n in range(2):
        window(1, n)
    edge_arrived(1)
    for n in range(2):
        window_edge(1, n)
    send_codes(1)

    mine = jnp.where(lo == hi, 0, 1)
    total[...] = part[mine, pl.ds(pl.multiple_of(block_rows(0), BLOCK), BLOCK), :]
    for slot in (9, 15, 1, 7, 8, 10, 14, 2, 6, 11, 13, 3, 5, 12, 4):
        pltpu.make_async_remote_copy(
            src_ref=landed.at[slot], dst_ref=landed.at[slot], send_sem=rs_recv.at[slot], recv_sem=rs_recv.at[slot],
            device_id=(tm, (rows + 1) % 16), device_id_type=MESH,
        ).wait_recv()
        power = landed[slot, pl.ds(4 * BLOCK, 16), :].astype(jnp.int32).astype(jnp.float32)
        scale = jnp.exp2(power * 0.0625) * (1.0 / CODES)
        scale = jnp.concatenate([jnp.broadcast_to(scale[4 * q:4 * q + 1], (8, 128)) for q in range(4)], 0)
        for g in range(4):
            values = landed[slot, pl.ds(g * BLOCK, BLOCK), :].astype(jnp.int32).astype(jnp.float32)
            total[:, pl.ds(g * 128, 128)] += values * scale
    env = total[...]
    result = out_turn[...] * env + out_cross[...] * swap_parts(env)
    for q in range(4):
        for p in range(2):
            out_ref[q, p] = result[q * 8 + p * 4:q * 8 + p * 4 + 4]

    for k in range(2):
        for d in range(1, 8):
            code_copy(k, d).wait_send()
    code_copy_left = pltpu.make_async_remote_copy(
        src_ref=codes.at[1 - mine, 0], dst_ref=landed.at[8], send_sem=rs_send.at[1 - mine, 0], recv_sem=rs_recv.at[8],
        device_id=(tm, (1 - lo) * 8 + z), device_id_type=MESH,
    )
    code_copy_left.wait_send()
    for copy in sends:
        copy.wait_send()

    @pl.when(tm > 0)
    def _():
        for half in range(2):
            edge_copy(half).wait_send()


def body(snapshots, spod_modes, freq_index, seg_offsets):
    bf16, f32 = jnp.bfloat16, jnp.float32
    vmem = pltpu.VMEM
    dma = pltpu.SemaphoreType.DMA
    return pl.pallas_call(
        kernel,
        out_shape=jax.ShapeDtypeStruct((F // 16, 2, M, S), f32),
        in_specs=[
            pl.BlockSpec(memory_space=pltpu.SMEM),
            pl.BlockSpec(memory_space=pl.ANY),
            pl.BlockSpec(memory_space=pl.ANY),
            pl.BlockSpec(memory_space=vmem),
        ],
        out_specs=pl.BlockSpec(memory_space=vmem),
        scratch_shapes=[
            vmem((T, R), bf16),
            vmem((2, HALF, R), bf16),
            vmem((2, HALF, T + L), bf16),
            vmem((2, HALF, T + L), bf16),
            vmem((T + L, S), bf16),
            vmem((T + L, S), bf16),
            vmem((2, HALF, L), f32),
            vmem((2, HALF, L), f32),
            vmem((L, S), f32),
            vmem((BLOCK, S), f32),
            vmem((BLOCK, S), f32),
            vmem((2, HALF, S), f32),
            vmem((2, 8, 4 * BLOCK + 16, 128), jnp.int16),
            vmem((16, 4 * BLOCK + 16, 128), jnp.int16),
            vmem((F // 16, 2, M, R), bf16),
            vmem((BLOCK, S), f32),
            vmem((2, HALF + 32, L), jnp.int16),
            vmem((2, HALF + 32, L), jnp.int16),
            dma, dma,
            dma((15,)), dma((16,)),
            dma((2,)), dma((2,)),
            dma((2, 8)), dma((16,)),
        ],
        compiler_params=pltpu.CompilerParams(
            collective_id=0, has_side_effects=True, vmem_limit_bytes=56 * 1024 * 1024
        ),
        cost_estimate=pl.CostEstimate(flops=8 * 10**9, bytes_accessed=10**7, transcendentals=0),
    )(freq_index, snapshots, spod_modes, seg_offsets.reshape(1, S))


def solution(mesh):
    placed = (P("tm", "rows"), P("tm", None, None, "rows"), P(), P("tm"))
    return jax.shard_map(
        body, mesh=mesh, in_specs=placed, out_specs=P("rows", None, None, "tm"), check_vma=False
    )
```

```python
import functools
import math

import jax
import jax.numpy as jnp
from jax import lax
from jax.experimental import pallas as pl
from jax.experimental.pallas import tpu as pltpu
from jax.sharding import PartitionSpec as P

F = 64
M = 4
L = 256
T = 2048
S = 512
R = 2048
BLOCK = 32
HALF = 256
TILES = T // L
SCALE = 2.0 * math.pi / L
PEAK = math.sqrt(8.0 / (3.0 * L))
CODES = 32767.0
MESH = pl.DeviceIdType.MESH
NT = (((1,), (1,)), ((), ()))


def swap_parts(x):
    rows, cols = x.shape
    return pltpu.roll(x.reshape(rows // 8, 8, cols), 4, 1).reshape(rows, cols)


def split(x):
    high = x.astype(jnp.bfloat16)
    return high, (x - high.astype(jnp.float32)).astype(jnp.bfloat16)


def dot(a, b):
    return jnp.dot(a, b, preferred_element_type=jnp.float32)


def to_codes(x):
    return jnp.round(x).astype(jnp.int32).astype(jnp.int16)


def from_codes(codes):
    return codes.astype(jnp.int32).astype(jnp.float32)


def power_above(largest):
    return jnp.ceil(16.0 * jnp.log2(jnp.maximum(largest, 1e-30))) + 1.0


def kernel(
    freq_ref, snap_hbm, modes_hbm, off_ref, out_ref,
    snap, modes, d_high, d_low, w_high, w_low, turn, cross, hann, out_turn, out_cross,
    part, codes, landed, relayed, raw, total, edge_out, edge_in,
    snap_sem, own_sem, ag_send, ag_recv, edge_send, edge_recv, rs_send, rs_recv, relay_recv,
):
    tm = lax.axis_index("tm")
    rows = lax.axis_index("rows")
    hi, y, core = tm // 8, (tm // 2) % 4, tm % 2
    lo, z = rows // 8, rows % 8
    way = 1 - 2 * core

    def block_id(h, yy, c):
        return h * 8 + (yy % 4) * 2 + c

    def at(b):
        return modes.at[b // 8, pl.ds(pl.multiple_of((b % 8) * BLOCK, BLOCK), BLOCK), :]

    snap_copy = pltpu.make_async_copy(snap_hbm, snap, snap_sem)
    snap_copy.start()
    own_copy = pltpu.make_async_copy(modes_hbm, raw, own_sem)
    own_copy.start()

    mate = block_id(hi, y, 1 - core)
    up, down, opposite = [block_id(hi, y + k, core) for k in (1, 3, 2)]
    peer, peer_up, peer_down, peer_opposite = [block_id(1 - hi, y + k, core) for k in (0, 1, 3, 2)]
    below = (tm + 15) % 16
    above = (tm + 1) % 16
    cross_edge = jnp.where(core == 0, below, above)

    barrier = pltpu.get_barrier_semaphore()
    for b in (mate, cross_edge, up, down, opposite, peer):
        pl.semaphore_signal(barrier, inc=1, device_id=(b, rows), device_id_type=MESH)
    for d in (1, 2, 6, 7):
        pl.semaphore_signal(barrier, inc=1, device_id=(tm, lo * 8 + (z + d) % 8), device_id_type=MESH)
    for d in (0, 1, 2, 6, 7):
        pl.semaphore_signal(barrier, inc=1, device_id=(tm, (1 - lo) * 8 + (z + d) % 8), device_id_type=MESH)

    lane = lax.broadcasted_iota(jnp.int32, (8, L), 1)
    upper = lax.broadcasted_iota(jnp.int32, (8, L), 0) < 4

    @pl.loop(0, F, unroll=4)
    def _(f):
        angle = ((freq_ref[f] * lane) & (L - 1)).astype(jnp.float32) * SCALE
        cosine = jnp.cos(angle)
        at_rows = pl.ds(pl.multiple_of((f % 32) * 8, 8), 8)
        turn[f // 32, at_rows, :] = jnp.where(upper, cosine, -cosine)
        cross[f // 32, at_rows, :] = -jnp.sin(angle)

    offsets = off_ref[...]
    upper_out = lax.broadcasted_iota(jnp.int32, (8, S), 0) < 4
    for q in range(4):
        bins = (freq_ref[rows * 4 + q] * jnp.broadcast_to(offsets, (8, S))) & (L - 1)
        angle = bins.astype(jnp.float32) * SCALE
        sine = jnp.sin(angle)
        out_turn[pl.ds(q * 8, 8), :] = jnp.cos(angle)
        out_cross[pl.ds(q * 8, 8), :] = jnp.where(upper_out, -sine, sine)

    within = offsets & (L - 1)
    tile_of = offsets // L

    @pl.loop(0, L // 32)
    def _(k):
        moment = k * 32 + lax.broadcasted_iota(jnp.int32, (32, S), 0)
        angle = ((moment - within) & (L - 1)).astype(jnp.float32) * SCALE
        hann[pl.ds(pl.multiple_of(k * 32, 32), 32), :] = PEAK * (0.5 - 0.5 * jnp.cos(angle))

    @pl.loop(0, TILES + 1)
    def _(tile):
        @pl.loop(0, L // 32)
        def _(k):
            moment = k * 32 + lax.broadcasted_iota(jnp.int32, (32, S), 0)
            start_tile = jnp.where(moment >= within, tile_of, tile_of + 1)
            values = hann[pl.ds(pl.multiple_of(k * 32, 32), 32), :]
            high, low = split(jnp.where(start_tile == tile, values, 0.0))
            here = pl.ds(pl.multiple_of(tile * L + k * 32, 32), 32)
            w_high[here, :] = high
            w_low[here, :] = low

    own_copy.wait()
    own = at(tm)
    for n in range(2):
        pair = [raw[2 * n + q].astype(jnp.float32).reshape(8, R) for q in range(2)]
        own[pl.ds(n * 16, 16), :] = jnp.concatenate(pair, 0).astype(jnp.bfloat16)

    pl.semaphore_wait(barrier, 15)

    sends = []

    def send(src, dst, send_sem, recv_sem, to):
        copy = pltpu.make_async_remote_copy(
            src_ref=src, dst_ref=dst, send_sem=send_sem, recv_sem=recv_sem, device_id=to, device_id_type=MESH
        )
        copy.start()
        sends.append(copy)

    def arrived(dst, recv_sem, to):
        pltpu.make_async_remote_copy(
            src_ref=dst, dst_ref=dst, send_sem=recv_sem, recv_sem=recv_sem, device_id=to, device_id_type=MESH
        ).wait_recv()

    def send_block(n, b, to):
        send(at(b), at(b), ag_send.at[n], ag_recv.at[b], (to, rows))

    def block_arrived(b, source):
        arrived(at(b), ag_recv.at[b], (source, rows))

    send_block(0, tm, opposite)
    send_block(1, tm, peer)
    send_block(2, tm, up)
    send_block(3, tm, down)
    send_block(4, tm, mate)
    block_arrived(opposite, opposite)
    send_block(5, opposite, peer)
    block_arrived(peer, peer)
    send_block(6, peer, up)
    send_block(7, peer, down)
    send_block(8, opposite, mate)
    block_arrived(up, up)
    send_block(9, up, mate)
    block_arrived(down, down)
    send_block(10, down, mate)
    send_block(11, peer, mate)

    snap_copy.wait()
    for k in (0, 2, 1, 3):
        block_arrived(block_id(hi, y + k, 1 - core), mate)

    def edge_copy(half):
        return pltpu.make_async_remote_copy(
            src_ref=edge_out.at[half], dst_ref=edge_in.at[half],
            send_sem=edge_send.at[half], recv_sem=edge_recv.at[half],
            device_id=(below, rows), device_id_type=MESH,
        )

    def half_of(k):
        return hi if k == 0 else 1 - hi

    def to_rows(x):
        return jnp.broadcast_to(x[:, None, :], (32, 8, 128)).reshape(HALF, 128)

    def project(k, tile):
        half = half_of(k)
        p = lax.dot_general(
            modes[half], snap[pl.ds(tile * L, L), :], NT, preferred_element_type=jnp.float32
        )
        d = turn[half] * p + cross[half] * swap_parts(p)
        if tile == 0:
            largest = jnp.max(jnp.abs(d), axis=1, keepdims=True)
            largest = jnp.max(jnp.broadcast_to(largest, (HALF, 128)).reshape(32, 8, 128), axis=1)
            power = power_above(largest)
            inverse = to_rows(CODES / jnp.exp2(power * 0.0625))
            edge_out[half, pl.ds(HALF, 32), :] = to_codes(jnp.concatenate([power] * 2, 1))
            edge_out[half, pl.ds(0, HALF), :] = to_codes(d * jnp.concatenate([inverse] * 2, 1))

            @pl.when(tm > 0)
            def _():
                edge_copy(half).start()

        high, low = split(d)
        d_high[half, :, pl.ds(tile * L, L)] = high
        d_low[half, :, pl.ds(tile * L, L)] = low

    def sums(half, first, length, cols):
        at_t = pl.ds(first, length)
        high = d_high[half, :, at_t]
        return (
            dot(high, w_high[at_t, cols])
            + dot(d_low[half, :, at_t], w_high[at_t, cols])
            + dot(high, w_low[at_t, cols])
        )

    def columns(n):
        return pl.ds(n * 256, 256)

    def window(k, n):
        part[k, :, columns(n)] = sums(half_of(k), 0, T, columns(n))

    def edge_arrived(k):
        half = half_of(k)

        @pl.when(tm < 15)
        def _():
            arrived(edge_in.at[half], edge_recv.at[half], (above, rows))
            power = from_codes(edge_in[half, pl.ds(HALF, 32), pl.ds(0, 128)])
            scale = to_rows(jnp.exp2(power * 0.0625) * (1.0 / CODES))
            values = from_codes(edge_in[half, pl.ds(0, HALF), :])
            high, low = split(values * jnp.concatenate([scale] * 2, 1))
            d_high[half, :, pl.ds(T, L)] = high
            d_low[half, :, pl.ds(T, L)] = low

    def window_edge(k, n):
        @pl.when(tm < 15)
        def _():
            part[k, :, columns(n)] += sums(half_of(k), T, L, columns(n))

    block_of = (4, 3, -3, 1, -1, 2, -2, 0)
    relay_of = (2, 1, -1)

    def along(d):
        return (z + 8 + d * way) % 8

    def block(d):
        return pl.ds(pl.multiple_of(along(d) * BLOCK, BLOCK), BLOCK)

    def encode(k, i):
        first = along(block_of[i]) * BLOCK
        powers = []
        for pair in range(2):
            scaled = []
            for q in (2 * pair, 2 * pair + 1):
                x = part[k, pl.ds(pl.multiple_of(first + q * 8, 8), 8), :]
                largest = jnp.max(jnp.abs(x), axis=(0, 1), keepdims=True)
                power = power_above(jnp.broadcast_to(largest, (8, 128)))
                inverse = CODES / jnp.exp2(power * 0.0625)
                scaled.append(x * jnp.concatenate([inverse] * 4, 1))
                powers.append(power[:4])
            pair_codes = to_codes(jnp.concatenate(scaled, 0))
            for g in range(4):
                codes[k, i, pl.ds(g * BLOCK + pair * 16, 16), :] = pair_codes[:, g * 128:(g + 1) * 128]
        codes[k, i, pl.ds(4 * BLOCK, 16), :] = to_codes(jnp.concatenate(powers, 0))

    def decode(ref):
        scale = jnp.exp2(from_codes(ref[pl.ds(4 * BLOCK, 16), :]) * 0.0625) * (1.0 / CODES)
        scale = jnp.concatenate([jnp.broadcast_to(scale[4 * q:4 * q + 1], (8, 128)) for q in range(4)], 0)
        return jnp.concatenate([from_codes(ref[pl.ds(g * BLOCK, BLOCK), :]) * scale for g in range(4)], 1)

    def code_copy(k, i):
        half = half_of(k)
        if i < 3:
            dst, recv_sem = relayed.at[k, i], relay_recv.at[k, i]
            owner = lo * 8 + along(relay_of[i])
        else:
            slot = jnp.where(lo == half, 0, 5) + i - 3
            dst, recv_sem = landed.at[slot], rs_recv.at[slot]
            owner = half * 8 + along(block_of[i])
        return pltpu.make_async_remote_copy(
            src_ref=codes.at[k, i], dst_ref=dst, send_sem=rs_send.at[k, i], recv_sem=recv_sem,
            device_id=(tm, owner), device_id_type=MESH,
        )

    def send_codes(k):
        for i in range(5):
            encode(k, i)
            code_copy(k, i).start()

        @pl.when(lo != half_of(k))
        def _():
            encode(k, 7)
            code_copy(k, 7).start()

    def relay(k):
        for i, sources in ((5, (1, 0)), (6, (2,))):
            for n in sources:
                arrived(relayed.at[k, n], relay_recv.at[k, n], (tm, lo * 8 + along(-relay_of[n])))
                part[k, block(block_of[i]), :] += decode(relayed.at[k, n])
            encode(k, i)
            code_copy(k, i).start()

    for tile in range(TILES):
        project(0, tile)
    for n, b in enumerate((peer_up, peer_down)):
        block_arrived(b, (up, down)[n])
        send_block(12 + n, b, mate)
    window(0, 0)
    block_arrived(peer_opposite, peer)
    send_block(14, peer_opposite, mate)
    window(0, 1)
    for k in (0, 1, 3, 2):
        block_arrived(block_id(1 - hi, y + k, 1 - core), mate)
    project(1, 0)
    project(1, 1)

    def finish_first():
        edge_arrived(0)
        for n in range(2):
            window_edge(0, n)
        send_codes(0)

    pl.when(tm != 7)(finish_first)
    for tile in range(2, TILES):
        project(1, tile)
    pl.when(tm == 7)(finish_first)
    for n in range(2):
        window(1, n)
    edge_arrived(1)
    for n in range(2):
        window_edge(1, n)
    send_codes(1)
    relay(0)
    relay(1)

    mine = jnp.where(lo == hi, 0, 1)
    total[...] = part[mine, block(0), :]
    for slot in (9, 0, 1, 5, 6, 2, 3, 7, 8):
        arrived(landed.at[slot], rs_recv.at[slot], (tm, lo * 8 + along(1)))
        total[...] += decode(landed.at[slot])
    env = total[...]
    result = out_turn[...] * env + out_cross[...] * swap_parts(env)
    for q in range(4):
        for p in range(2):
            out_ref[q, p] = result[q * 8 + p * 4:q * 8 + p * 4 + 4]

    for k in range(2):
        for i in range(7):
            code_copy(k, i).wait_send()
    pltpu.make_async_remote_copy(
        src_ref=codes.at[1 - mine, 7], dst_ref=landed.at[9], send_sem=rs_send.at[1 - mine, 7], recv_sem=rs_recv.at[9],
        device_id=(tm, (1 - lo) * 8 + z), device_id_type=MESH,
    ).wait_send()
    for copy in sends:
        copy.wait_send()

    @pl.when(tm > 0)
    def _():
        for half in range(2):
            edge_copy(half).wait_send()


def body(snapshots, spod_modes, freq_index, seg_offsets):
    bf16, f32 = jnp.bfloat16, jnp.float32
    vmem = pltpu.VMEM
    dma = pltpu.SemaphoreType.DMA
    return pl.pallas_call(
        kernel,
        out_shape=vmem((F // 16, 2, M, S), f32),
        in_specs=[
            pl.BlockSpec(memory_space=pltpu.SMEM),
            pl.BlockSpec(memory_space=pl.ANY),
            pl.BlockSpec(memory_space=pl.ANY),
            pl.BlockSpec(memory_space=vmem),
        ],
        out_specs=pl.BlockSpec(memory_space=vmem),
        scratch_shapes=[
            vmem((T, R), bf16),
            vmem((2, HALF, R), bf16),
            vmem((2, HALF, T + L), bf16),
            vmem((2, HALF, T + L), bf16),
            vmem((T + L, S), bf16),
            vmem((T + L, S), bf16),
            vmem((2, HALF, L), f32),
            vmem((2, HALF, L), f32),
            vmem((L, S), f32),
            vmem((BLOCK, S), f32),
            vmem((BLOCK, S), f32),
            vmem((2, HALF, S), f32),
            vmem((2, 8, 4 * BLOCK + 16, 128), jnp.int16),
            vmem((10, 4 * BLOCK + 16, 128), jnp.int16),
            vmem((2, 3, 4 * BLOCK + 16, 128), jnp.int16),
            vmem((F // 16, 2, M, R), bf16),
            vmem((BLOCK, S), f32),
            vmem((2, HALF + 32, L), jnp.int16),
            vmem((2, HALF + 32, L), jnp.int16),
            dma, dma,
            dma((15,)), dma((16,)),
            dma((2,)), dma((2,)),
            dma((2, 8)), dma((10,)), dma((2, 3)),
        ],
        compiler_params=pltpu.CompilerParams(
            collective_id=0, has_side_effects=True, vmem_limit_bytes=56 * 1024 * 1024
        ),
        cost_estimate=pl.CostEstimate(flops=8 * 10**9, bytes_accessed=10**7, transcendentals=0),
    )(freq_index, snapshots, spod_modes, seg_offsets.reshape(1, S))


def solution(mesh):
    placed = (P("tm", "rows"), P("tm", None, None, "rows"), P(), P("tm"))
    return jax.shard_map(
        body, mesh=mesh, in_specs=placed, out_specs=P("rows", None, None, "tm"), check_vma=False
    )
```

```python
import functools
import math

import jax
import jax.numpy as jnp
from jax import lax
from jax.experimental import pallas as pl
from jax.experimental.pallas import tpu as pltpu
from jax.sharding import PartitionSpec as P

F = 64
M = 4
L = 256
T = 2048
S = 512
R = 2048
BLOCK = 32
HALF = 256
TILES = T // L
SCALE = 2.0 * math.pi / L
PEAK = math.sqrt(8.0 / (3.0 * L))
CODES = 32767.0
MESH = pl.DeviceIdType.MESH
NT = (((1,), (1,)), ((), ()))


def swap_parts(x):
    rows, cols = x.shape
    return pltpu.roll(x.reshape(rows // 8, 8, cols), 4, 1).reshape(rows, cols)


def split(x):
    high = x.astype(jnp.bfloat16)
    return high, (x - high.astype(jnp.float32)).astype(jnp.bfloat16)


def dot(a, b):
    return jnp.dot(a, b, preferred_element_type=jnp.float32)


def to_codes(x):
    return jnp.round(x).astype(jnp.int32).astype(jnp.int16)


def from_codes(codes):
    return codes.astype(jnp.int32).astype(jnp.float32)


def power_above(largest):
    return jnp.ceil(16.0 * jnp.log2(jnp.maximum(largest, 1e-30))) + 1.0


def kernel(
    freq_ref, snap_hbm, modes_hbm, off_ref, out_ref,
    snap, modes, d_high, d_low, w_high, w_low, turn, cross, hann, out_turn, out_cross,
    part, codes, landed, relayed, raw, total, edge_out, edge_in,
    snap_sem, own_sem, ag_send, ag_recv, edge_send, edge_recv, rs_send, rs_recv, relay_recv,
):
    tm = lax.axis_index("tm")
    rows = lax.axis_index("rows")
    hi, y, core = tm // 8, (tm // 2) % 4, tm % 2
    lo, z = rows // 8, rows % 8
    way = 1 - 2 * core

    def block_id(h, yy, c):
        return h * 8 + (yy % 4) * 2 + c

    def at(b):
        return modes.at[b // 8, pl.ds(pl.multiple_of((b % 8) * BLOCK, BLOCK), BLOCK), :]

    snap_copy = pltpu.make_async_copy(snap_hbm, snap, snap_sem)
    snap_copy.start()
    own_copy = pltpu.make_async_copy(modes_hbm, raw, own_sem)
    own_copy.start()

    mate = block_id(hi, y, 1 - core)
    up, down, opposite = [block_id(hi, y + k, core) for k in (1, 3, 2)]
    peer, peer_up, peer_down, peer_opposite = [block_id(1 - hi, y + k, core) for k in (0, 1, 3, 2)]
    below = (tm + 15) % 16
    above = (tm + 1) % 16
    cross_edge = jnp.where(core == 0, below, above)

    barrier = pltpu.get_barrier_semaphore()
    for b in (mate, cross_edge, up, down, opposite, peer):
        pl.semaphore_signal(barrier, inc=1, device_id=(b, rows), device_id_type=MESH)
    for d in (1, 2, 6, 7):
        pl.semaphore_signal(barrier, inc=1, device_id=(tm, lo * 8 + (z + d) % 8), device_id_type=MESH)
    for d in (0, 1, 2, 6, 7):
        pl.semaphore_signal(barrier, inc=1, device_id=(tm, (1 - lo) * 8 + (z + d) % 8), device_id_type=MESH)

    lane = lax.broadcasted_iota(jnp.int32, (8, L), 1)
    upper = lax.broadcasted_iota(jnp.int32, (8, L), 0) < 4

    @pl.loop(0, F, unroll=4)
    def _(f):
        angle = ((freq_ref[f] * lane) & (L - 1)).astype(jnp.float32) * SCALE
        cosine = jnp.cos(angle)
        at_rows = pl.ds(pl.multiple_of((f % 32) * 8, 8), 8)
        turn[f // 32, at_rows, :] = jnp.where(upper, cosine, -cosine)
        cross[f // 32, at_rows, :] = -jnp.sin(angle)

    offsets = off_ref[...]
    upper_out = lax.broadcasted_iota(jnp.int32, (8, S), 0) < 4
    for q in range(4):
        bins = (freq_ref[rows * 4 + q] * jnp.broadcast_to(offsets, (8, S))) & (L - 1)
        angle = bins.astype(jnp.float32) * SCALE
        sine = jnp.sin(angle)
        out_turn[pl.ds(q * 8, 8), :] = jnp.cos(angle)
        out_cross[pl.ds(q * 8, 8), :] = jnp.where(upper_out, -sine, sine)

    within = offsets & (L - 1)
    tile_of = offsets // L

    @pl.loop(0, L // 32)
    def _(k):
        moment = k * 32 + lax.broadcasted_iota(jnp.int32, (32, S), 0)
        angle = ((moment - within) & (L - 1)).astype(jnp.float32) * SCALE
        hann[pl.ds(pl.multiple_of(k * 32, 32), 32), :] = PEAK * (0.5 - 0.5 * jnp.cos(angle))

    @pl.loop(0, TILES + 1)
    def _(tile):
        @pl.loop(0, L // 32)
        def _(k):
            moment = k * 32 + lax.broadcasted_iota(jnp.int32, (32, S), 0)
            start_tile = jnp.where(moment >= within, tile_of, tile_of + 1)
            values = hann[pl.ds(pl.multiple_of(k * 32, 32), 32), :]
            high, low = split(jnp.where(start_tile == tile, values, 0.0))
            here = pl.ds(pl.multiple_of(tile * L + k * 32, 32), 32)
            w_high[here, :] = high
            w_low[here, :] = low

    own_copy.wait()
    own = at(tm)
    for n in range(2):
        pair = [raw[2 * n + q].astype(jnp.float32).reshape(8, R) for q in range(2)]
        own[pl.ds(n * 16, 16), :] = jnp.concatenate(pair, 0).astype(jnp.bfloat16)

    pl.semaphore_wait(barrier, 15)

    sends = []

    def send(src, dst, send_sem, recv_sem, to):
        copy = pltpu.make_async_remote_copy(
            src_ref=src, dst_ref=dst, send_sem=send_sem, recv_sem=recv_sem, device_id=to, device_id_type=MESH
        )
        copy.start()
        sends.append(copy)

    def arrived(dst, recv_sem, to):
        pltpu.make_async_remote_copy(
            src_ref=dst, dst_ref=dst, send_sem=recv_sem, recv_sem=recv_sem, device_id=to, device_id_type=MESH
        ).wait_recv()

    def send_block(n, b, to):
        send(at(b), at(b), ag_send.at[n], ag_recv.at[b], (to, rows))

    def block_arrived(b, source):
        arrived(at(b), ag_recv.at[b], (source, rows))

    send_block(0, tm, opposite)
    send_block(1, tm, peer)
    send_block(2, tm, up)
    send_block(3, tm, down)
    send_block(4, tm, mate)
    block_arrived(opposite, opposite)
    send_block(5, opposite, peer)
    block_arrived(peer, peer)
    send_block(6, peer, up)
    send_block(7, peer, down)
    send_block(8, opposite, mate)
    block_arrived(up, up)
    send_block(9, up, mate)
    block_arrived(down, down)
    send_block(10, down, mate)
    send_block(11, peer, mate)

    snap_copy.wait()
    for k in (0, 2, 1, 3):
        block_arrived(block_id(hi, y + k, 1 - core), mate)

    def edge_copy(half):
        return pltpu.make_async_remote_copy(
            src_ref=edge_out.at[half], dst_ref=edge_in.at[half],
            send_sem=edge_send.at[half], recv_sem=edge_recv.at[half],
            device_id=(below, rows), device_id_type=MESH,
        )

    def half_of(k):
        return hi if k == 0 else 1 - hi

    def to_rows(x):
        return jnp.broadcast_to(x[:, None, :], (32, 8, 128)).reshape(HALF, 128)

    def project(k, tile):
        half = half_of(k)
        p = lax.dot_general(
            modes[half], snap[pl.ds(tile * L, L), :], NT, preferred_element_type=jnp.float32
        )
        d = turn[half] * p + cross[half] * swap_parts(p)
        if tile == 0:
            largest = jnp.max(jnp.abs(d), axis=1, keepdims=True)
            largest = jnp.max(jnp.broadcast_to(largest, (HALF, 128)).reshape(32, 8, 128), axis=1)
            power = power_above(largest)
            inverse = to_rows(CODES / jnp.exp2(power * 0.0625))
            edge_out[half, pl.ds(HALF, 32), :] = to_codes(jnp.concatenate([power] * 2, 1))
            edge_out[half, pl.ds(0, HALF), :] = to_codes(d * jnp.concatenate([inverse] * 2, 1))

            @pl.when(tm > 0)
            def _():
                edge_copy(half).start()

        high, low = split(d)
        d_high[half, :, pl.ds(tile * L, L)] = high
        d_low[half, :, pl.ds(tile * L, L)] = low

    def sums(half, first, length, cols):
        at_t = pl.ds(first, length)
        high = d_high[half, :, at_t]
        return (
            dot(high, w_high[at_t, cols])
            + dot(d_low[half, :, at_t], w_high[at_t, cols])
            + dot(high, w_low[at_t, cols])
        )

    def columns(n):
        return pl.ds(n * 256, 256)

    def window(k, n):
        part[k, :, columns(n)] = sums(half_of(k), 0, T, columns(n))

    def edge_arrived(k):
        half = half_of(k)

        @pl.when(tm < 15)
        def _():
            arrived(edge_in.at[half], edge_recv.at[half], (above, rows))
            power = from_codes(edge_in[half, pl.ds(HALF, 32), pl.ds(0, 128)])
            scale = to_rows(jnp.exp2(power * 0.0625) * (1.0 / CODES))
            values = from_codes(edge_in[half, pl.ds(0, HALF), :])
            high, low = split(values * jnp.concatenate([scale] * 2, 1))
            d_high[half, :, pl.ds(T, L)] = high
            d_low[half, :, pl.ds(T, L)] = low

    def window_edge(k, n):
        @pl.when(tm < 15)
        def _():
            part[k, :, columns(n)] += sums(half_of(k), T, L, columns(n))

    block_of = (4, 3, -3, 1, -1, 2, -2, 0)
    relay_of = (2, 1, -1)

    def along(d):
        return (z + 8 + d * way) % 8

    def block(d):
        return pl.ds(pl.multiple_of(along(d) * BLOCK, BLOCK), BLOCK)

    def encode(k, i):
        first = along(block_of[i]) * BLOCK
        powers = []
        for pair in range(2):
            scaled = []
            for q in (2 * pair, 2 * pair + 1):
                x = part[k, pl.ds(pl.multiple_of(first + q * 8, 8), 8), :]
                largest = jnp.max(jnp.abs(x), axis=(0, 1), keepdims=True)
                power = power_above(jnp.broadcast_to(largest, (8, 128)))
                inverse = CODES / jnp.exp2(power * 0.0625)
                scaled.append(x * jnp.concatenate([inverse] * 4, 1))
                powers.append(power[:4])
            pair_codes = to_codes(jnp.concatenate(scaled, 0))
            for g in range(4):
                codes[k, i, pl.ds(g * BLOCK + pair * 16, 16), :] = pair_codes[:, g * 128:(g + 1) * 128]
        codes[k, i, pl.ds(4 * BLOCK, 16), :] = to_codes(jnp.concatenate(powers, 0))

    def decode(ref):
        scale = jnp.exp2(from_codes(ref[pl.ds(4 * BLOCK, 16), :]) * 0.0625) * (1.0 / CODES)
        scale = jnp.concatenate([jnp.broadcast_to(scale[4 * q:4 * q + 1], (8, 128)) for q in range(4)], 0)
        return jnp.concatenate([from_codes(ref[pl.ds(g * BLOCK, BLOCK), :]) * scale for g in range(4)], 1)

    def code_copy(k, i):
        half = half_of(k)
        if i < 3:
            dst, recv_sem = relayed.at[k, i], relay_recv.at[k, i]
            owner = lo * 8 + along(relay_of[i])
        else:
            slot = jnp.where(lo == half, 0, 5) + i - 3
            dst, recv_sem = landed.at[slot], rs_recv.at[slot]
            owner = half * 8 + along(block_of[i])
        return pltpu.make_async_remote_copy(
            src_ref=codes.at[k, i], dst_ref=dst, send_sem=rs_send.at[k, i], recv_sem=recv_sem,
            device_id=(tm, owner), device_id_type=MESH,
        )

    def send_codes(k):
        for group in ((0, 1, 2), (3, 4)):
            for i in group:
                encode(k, i)
            for i in group:
                code_copy(k, i).start()

        @pl.when(lo != half_of(k))
        def _():
            encode(k, 7)
            code_copy(k, 7).start()

    def relay(k):
        for i, sources in ((5, (1, 0)), (6, (2,))):
            for n in sources:
                arrived(relayed.at[k, n], relay_recv.at[k, n], (tm, lo * 8 + along(-relay_of[n])))
                part[k, block(block_of[i]), :] += decode(relayed.at[k, n])
            encode(k, i)
            code_copy(k, i).start()

    for tile in range(TILES):
        project(0, tile)
        if tile == 4:
            for n, b in enumerate((peer_up, peer_down)):
                block_arrived(b, (up, down)[n])
                send_block(12 + n, b, mate)
    block_arrived(peer_opposite, peer)
    send_block(14, peer_opposite, mate)
    window(0, 0)
    window(0, 1)
    for k in (0, 1, 3, 2):
        block_arrived(block_id(1 - hi, y + k, 1 - core), mate)
    project(1, 0)
    project(1, 1)

    def finish_first():
        edge_arrived(0)
        for n in range(2):
            window_edge(0, n)
        send_codes(0)

    pl.when(tm != 7)(finish_first)
    for tile in range(2, TILES):
        project(1, tile)
    pl.when(tm == 7)(finish_first)
    for n in range(2):
        window(1, n)
    edge_arrived(1)
    for n in range(2):
        window_edge(1, n)
    send_codes(1)
    relay(0)
    relay(1)

    mine = jnp.where(lo == hi, 0, 1)
    total[...] = part[mine, block(0), :]
    for slot in (9, 0, 1, 5, 6, 2, 3, 7, 8):
        arrived(landed.at[slot], rs_recv.at[slot], (tm, lo * 8 + along(1)))
        total[...] += decode(landed.at[slot])
    env = total[...]
    result = out_turn[...] * env + out_cross[...] * swap_parts(env)
    for q in range(4):
        for p in range(2):
            out_ref[q, p] = result[q * 8 + p * 4:q * 8 + p * 4 + 4]

    for k in range(2):
        for i in range(7):
            code_copy(k, i).wait_send()
    pltpu.make_async_remote_copy(
        src_ref=codes.at[1 - mine, 7], dst_ref=landed.at[9], send_sem=rs_send.at[1 - mine, 7], recv_sem=rs_recv.at[9],
        device_id=(tm, (1 - lo) * 8 + z), device_id_type=MESH,
    ).wait_send()
    for copy in sends:
        copy.wait_send()

    @pl.when(tm > 0)
    def _():
        for half in range(2):
            edge_copy(half).wait_send()


def body(snapshots, spod_modes, freq_index, seg_offsets):
    bf16, f32 = jnp.bfloat16, jnp.float32
    vmem = pltpu.VMEM
    dma = pltpu.SemaphoreType.DMA
    return pl.pallas_call(
        kernel,
        out_shape=vmem((F // 16, 2, M, S), f32),
        in_specs=[
            pl.BlockSpec(memory_space=pltpu.SMEM),
            pl.BlockSpec(memory_space=pl.ANY),
            pl.BlockSpec(memory_space=pl.ANY),
            pl.BlockSpec(memory_space=vmem),
        ],
        out_specs=pl.BlockSpec(memory_space=vmem),
        scratch_shapes=[
            vmem((T, R), bf16),
            vmem((2, HALF, R), bf16),
            vmem((2, HALF, T + L), bf16),
            vmem((2, HALF, T + L), bf16),
            vmem((T + L, S), bf16),
            vmem((T + L, S), bf16),
            vmem((2, HALF, L), f32),
            vmem((2, HALF, L), f32),
            vmem((L, S), f32),
            vmem((BLOCK, S), f32),
            vmem((BLOCK, S), f32),
            vmem((2, HALF, S), f32),
            vmem((2, 8, 4 * BLOCK + 16, 128), jnp.int16),
            vmem((10, 4 * BLOCK + 16, 128), jnp.int16),
            vmem((2, 3, 4 * BLOCK + 16, 128), jnp.int16),
            vmem((F // 16, 2, M, R), bf16),
            vmem((BLOCK, S), f32),
            vmem((2, HALF + 32, L), jnp.int16),
            vmem((2, HALF + 32, L), jnp.int16),
            dma, dma,
            dma((15,)), dma((16,)),
            dma((2,)), dma((2,)),
            dma((2, 8)), dma((10,)), dma((2, 3)),
        ],
        compiler_params=pltpu.CompilerParams(
            collective_id=0, has_side_effects=True, vmem_limit_bytes=56 * 1024 * 1024
        ),
        cost_estimate=pl.CostEstimate(flops=8 * 10**9, bytes_accessed=10**7, transcendentals=0),
    )(freq_index, snapshots, spod_modes, seg_offsets.reshape(1, S))


def solution(mesh):
    placed = (P("tm", "rows"), P("tm", None, None, "rows"), P(), P("tm"))
    return jax.shard_map(
        body, mesh=mesh, in_specs=placed, out_specs=P("rows", None, None, "tm"), check_vma=False
    )
```

```python
import functools
import math

import jax
import jax.numpy as jnp
from jax import lax
from jax.experimental import pallas as pl
from jax.experimental.pallas import tpu as pltpu
from jax.sharding import PartitionSpec as P

F = 64
M = 4
L = 256
T = 2048
S = 512
R = 2048
BLOCK = 32
HALF = 256
TILES = T // L
SCALE = 2.0 * math.pi / L
PEAK = math.sqrt(8.0 / (3.0 * L))
CODES = 32767.0
MESH = pl.DeviceIdType.MESH
NT = (((1,), (1,)), ((), ()))


def swap_parts(x):
    rows, cols = x.shape
    return pltpu.roll(x.reshape(rows // 8, 8, cols), 4, 1).reshape(rows, cols)


def split(x):
    high = x.astype(jnp.bfloat16)
    return high, (x - high.astype(jnp.float32)).astype(jnp.bfloat16)


def dot(a, b):
    return jnp.dot(a, b, preferred_element_type=jnp.float32)


def to_codes(x):
    return jnp.round(x).astype(jnp.int32).astype(jnp.int16)


def from_codes(codes):
    return codes.astype(jnp.int32).astype(jnp.float32)


def power_above(largest):
    return jnp.ceil(16.0 * jnp.log2(jnp.maximum(largest, 1e-30))) + 1.0


def kernel(
    freq_ref, snap_hbm, modes_hbm, off_ref, out_ref,
    snap, modes, d_high, d_low, w_high, w_low, turn, cross, hann, out_turn, out_cross,
    part, codes, landed, relayed, raw, total, edge_out, edge_in,
    snap_sem, own_sem, ag_send, ag_recv, edge_send, edge_recv, rs_send, rs_recv, relay_recv,
):
    tm = lax.axis_index("tm")
    rows = lax.axis_index("rows")
    hi, y, core = tm // 8, (tm // 2) % 4, tm % 2
    lo, z = rows // 8, rows % 8
    way = 1 - 2 * core

    def block_id(h, yy, c):
        return h * 8 + (yy % 4) * 2 + c

    def at(b):
        return modes.at[b // 8, pl.ds(pl.multiple_of((b % 8) * BLOCK, BLOCK), BLOCK), :]

    snap_copy = pltpu.make_async_copy(snap_hbm, snap, snap_sem)
    snap_copy.start()
    own_copy = pltpu.make_async_copy(modes_hbm, raw, own_sem)
    own_copy.start()

    mate = block_id(hi, y, 1 - core)
    up, down, opposite = [block_id(hi, y + k, core) for k in (1, 3, 2)]
    peer, peer_up, peer_down, peer_opposite = [block_id(1 - hi, y + k, core) for k in (0, 1, 3, 2)]
    below = (tm + 15) % 16
    above = (tm + 1) % 16
    cross_edge = jnp.where(core == 0, below, above)

    barrier = pltpu.get_barrier_semaphore()
    for b in (mate, cross_edge, up, down, opposite, peer):
        pl.semaphore_signal(barrier, inc=1, device_id=(b, rows), device_id_type=MESH)
    for d in (1, 2, 6, 7):
        pl.semaphore_signal(barrier, inc=1, device_id=(tm, lo * 8 + (z + d) % 8), device_id_type=MESH)
    for d in (0, 1, 2, 6, 7):
        pl.semaphore_signal(barrier, inc=1, device_id=(tm, (1 - lo) * 8 + (z + d) % 8), device_id_type=MESH)

    lane = lax.broadcasted_iota(jnp.int32, (8, L), 1)
    upper = lax.broadcasted_iota(jnp.int32, (8, L), 0) < 4

    @pl.loop(0, F, unroll=4)
    def _(f):
        angle = ((freq_ref[f] * lane) & (L - 1)).astype(jnp.float32) * SCALE
        cosine = jnp.cos(angle)
        at_rows = pl.ds(pl.multiple_of((f % 32) * 8, 8), 8)
        turn[f // 32, at_rows, :] = jnp.where(upper, cosine, -cosine)
        cross[f // 32, at_rows, :] = -jnp.sin(angle)

    offsets = off_ref[...]
    upper_out = lax.broadcasted_iota(jnp.int32, (8, S), 0) < 4
    for q in range(4):
        bins = (freq_ref[rows * 4 + q] * jnp.broadcast_to(offsets, (8, S))) & (L - 1)
        angle = bins.astype(jnp.float32) * SCALE
        sine = jnp.sin(angle)
        out_turn[pl.ds(q * 8, 8), :] = jnp.cos(angle)
        out_cross[pl.ds(q * 8, 8), :] = jnp.where(upper_out, -sine, sine)

    within = offsets & (L - 1)
    tile_of = offsets // L

    @pl.loop(0, L // 32)
    def _(k):
        moment = k * 32 + lax.broadcasted_iota(jnp.int32, (32, S), 0)
        angle = ((moment - within) & (L - 1)).astype(jnp.float32) * SCALE
        hann[pl.ds(pl.multiple_of(k * 32, 32), 32), :] = PEAK * (0.5 - 0.5 * jnp.cos(angle))

    @pl.loop(0, TILES + 1)
    def _(tile):
        @pl.loop(0, L // 32)
        def _(k):
            moment = k * 32 + lax.broadcasted_iota(jnp.int32, (32, S), 0)
            start_tile = jnp.where(moment >= within, tile_of, tile_of + 1)
            values = hann[pl.ds(pl.multiple_of(k * 32, 32), 32), :]
            high, low = split(jnp.where(start_tile == tile, values, 0.0))
            here = pl.ds(pl.multiple_of(tile * L + k * 32, 32), 32)
            w_high[here, :] = high
            w_low[here, :] = low

    own_copy.wait()
    own = at(tm)
    for n in range(2):
        pair = [raw[2 * n + q].astype(jnp.float32).reshape(8, R) for q in range(2)]
        own[pl.ds(n * 16, 16), :] = jnp.concatenate(pair, 0).astype(jnp.bfloat16)

    pl.semaphore_wait(barrier, 15)

    sends = []

    def send(src, dst, send_sem, recv_sem, to):
        copy = pltpu.make_async_remote_copy(
            src_ref=src, dst_ref=dst, send_sem=send_sem, recv_sem=recv_sem, device_id=to, device_id_type=MESH
        )
        copy.start()
        sends.append(copy)

    def arrived(dst, recv_sem, to):
        pltpu.make_async_remote_copy(
            src_ref=dst, dst_ref=dst, send_sem=recv_sem, recv_sem=recv_sem, device_id=to, device_id_type=MESH
        ).wait_recv()

    def send_block(n, b, to):
        send(at(b), at(b), ag_send.at[n], ag_recv.at[b], (to, rows))

    def block_arrived(b, source):
        arrived(at(b), ag_recv.at[b], (source, rows))

    send_block(0, tm, opposite)
    send_block(1, tm, peer)
    send_block(2, tm, up)
    send_block(3, tm, down)
    send_block(4, tm, mate)
    block_arrived(peer, peer)
    send_block(6, peer, up)
    send_block(7, peer, down)
    block_arrived(opposite, opposite)
    send_block(5, opposite, peer)
    send_block(8, opposite, mate)
    block_arrived(up, up)
    send_block(9, up, mate)
    block_arrived(down, down)
    send_block(10, down, mate)
    send_block(11, peer, mate)

    snap_copy.wait()
    for k in (0, 2, 1, 3):
        block_arrived(block_id(hi, y + k, 1 - core), mate)

    def edge_copy(half):
        return pltpu.make_async_remote_copy(
            src_ref=edge_out.at[half], dst_ref=edge_in.at[half],
            send_sem=edge_send.at[half], recv_sem=edge_recv.at[half],
            device_id=(below, rows), device_id_type=MESH,
        )

    def half_of(k):
        return hi if k == 0 else 1 - hi

    def to_rows(x):
        return jnp.broadcast_to(x[:, None, :], (32, 8, 128)).reshape(HALF, 128)

    def project(k, tile):
        half = half_of(k)
        p = lax.dot_general(
            modes[half], snap[pl.ds(tile * L, L), :], NT, preferred_element_type=jnp.float32
        )
        d = turn[half] * p + cross[half] * swap_parts(p)
        if tile == 0:
            largest = jnp.max(jnp.abs(d), axis=1, keepdims=True)
            largest = jnp.max(jnp.broadcast_to(largest, (HALF, 128)).reshape(32, 8, 128), axis=1)
            power = power_above(largest)
            inverse = to_rows(CODES / jnp.exp2(power * 0.0625))
            edge_out[half, pl.ds(HALF, 32), :] = to_codes(jnp.concatenate([power] * 2, 1))
            edge_out[half, pl.ds(0, HALF), :] = to_codes(d * jnp.concatenate([inverse] * 2, 1))

            @pl.when(tm > 0)
            def _():
                edge_copy(half).start()

        high, low = split(d)
        d_high[half, :, pl.ds(tile * L, L)] = high
        d_low[half, :, pl.ds(tile * L, L)] = low

    def sums(half, first, length, cols):
        at_t = pl.ds(first, length)
        high = d_high[half, :, at_t]
        return (
            dot(high, w_high[at_t, cols])
            + dot(d_low[half, :, at_t], w_high[at_t, cols])
            + dot(high, w_low[at_t, cols])
        )

    def columns(n):
        return pl.ds(n * 256, 256)

    def window(k, n):
        part[k, :, columns(n)] = sums(half_of(k), 0, T, columns(n))

    def edge_arrived(k):
        half = half_of(k)

        @pl.when(tm < 15)
        def _():
            arrived(edge_in.at[half], edge_recv.at[half], (above, rows))
            power = from_codes(edge_in[half, pl.ds(HALF, 32), pl.ds(0, 128)])
            scale = to_rows(jnp.exp2(power * 0.0625) * (1.0 / CODES))
            values = from_codes(edge_in[half, pl.ds(0, HALF), :])
            high, low = split(values * jnp.concatenate([scale] * 2, 1))
            d_high[half, :, pl.ds(T, L)] = high
            d_low[half, :, pl.ds(T, L)] = low

    def window_edge(k, n):
        @pl.when(tm < 15)
        def _():
            part[k, :, columns(n)] += sums(half_of(k), T, L, columns(n))

    block_of = (4, 3, -3, 1, -1, 2, -2, 0)
    relay_of = (2, 1, -1)

    def along(d):
        return (z + 8 + d * way) % 8

    def block(d):
        return pl.ds(pl.multiple_of(along(d) * BLOCK, BLOCK), BLOCK)

    def encode(k, i):
        first = along(block_of[i]) * BLOCK
        powers = []
        for pair in range(2):
            scaled = []
            for q in (2 * pair, 2 * pair + 1):
                x = part[k, pl.ds(pl.multiple_of(first + q * 8, 8), 8), :]
                largest = jnp.max(jnp.abs(x), axis=(0, 1), keepdims=True)
                power = power_above(jnp.broadcast_to(largest, (8, 128)))
                inverse = CODES / jnp.exp2(power * 0.0625)
                scaled.append(x * jnp.concatenate([inverse] * 4, 1))
                powers.append(power[:4])
            pair_codes = to_codes(jnp.concatenate(scaled, 0))
            for g in range(4):
                codes[k, i, pl.ds(g * BLOCK + pair * 16, 16), :] = pair_codes[:, g * 128:(g + 1) * 128]
        codes[k, i, pl.ds(4 * BLOCK, 16), :] = to_codes(jnp.concatenate(powers, 0))

    def decode(ref):
        scale = jnp.exp2(from_codes(ref[pl.ds(4 * BLOCK, 16), :]) * 0.0625) * (1.0 / CODES)
        scale = jnp.concatenate([jnp.broadcast_to(scale[4 * q:4 * q + 1], (8, 128)) for q in range(4)], 0)
        return jnp.concatenate([from_codes(ref[pl.ds(g * BLOCK, BLOCK), :]) * scale for g in range(4)], 1)

    def code_copy(k, i):
        half = half_of(k)
        if i < 3:
            dst, recv_sem = relayed.at[k, i], relay_recv.at[k, i]
            owner = lo * 8 + along(relay_of[i])
        else:
            slot = jnp.where(lo == half, 0, 5) + i - 3
            dst, recv_sem = landed.at[slot], rs_recv.at[slot]
            owner = half * 8 + along(block_of[i])
        return pltpu.make_async_remote_copy(
            src_ref=codes.at[k, i], dst_ref=dst, send_sem=rs_send.at[k, i], recv_sem=recv_sem,
            device_id=(tm, owner), device_id_type=MESH,
        )

    def send_codes(k):
        for group in ((0, 1, 2), (3, 4)):
            for i in group:
                encode(k, i)
            for i in group:
                code_copy(k, i).start()

        @pl.when(lo != half_of(k))
        def _():
            encode(k, 7)
            code_copy(k, 7).start()

    def relay(k):
        for i, sources in ((6, (2,)), (5, (1, 0))):
            for n in sources:
                arrived(relayed.at[k, n], relay_recv.at[k, n], (tm, lo * 8 + along(-relay_of[n])))
                part[k, block(block_of[i]), :] += decode(relayed.at[k, n])
            encode(k, i)
            code_copy(k, i).start()

    for tile in range(TILES):
        project(0, tile)
        if tile == 4:
            for n, b in enumerate((peer_up, peer_down)):
                block_arrived(b, (up, down)[n])
                send_block(12 + n, b, mate)
    block_arrived(peer_opposite, peer)
    send_block(14, peer_opposite, mate)
    window(0, 0)
    window(0, 1)
    for k in (0, 1, 3, 2):
        block_arrived(block_id(1 - hi, y + k, 1 - core), mate)
    project(1, 0)
    project(1, 1)

    def finish_first():
        edge_arrived(0)
        for n in range(2):
            window_edge(0, n)
        send_codes(0)

    pl.when(tm != 7)(finish_first)
    for tile in range(2, TILES):
        project(1, tile)
    pl.when(tm == 7)(finish_first)
    for n in range(2):
        window(1, n)
    edge_arrived(1)
    for n in range(2):
        window_edge(1, n)
    send_codes(1)
    relay(0)
    relay(1)

    mine = jnp.where(lo == hi, 0, 1)
    total[...] = part[mine, block(0), :]
    for slot in (9, 0, 1, 5, 6, 2, 3, 7, 8):
        arrived(landed.at[slot], rs_recv.at[slot], (tm, lo * 8 + along(1)))
        total[...] += decode(landed.at[slot])
    env = total[...]
    result = out_turn[...] * env + out_cross[...] * swap_parts(env)
    for q in range(4):
        for p in range(2):
            out_ref[q, p] = result[q * 8 + p * 4:q * 8 + p * 4 + 4]

    for k in range(2):
        for i in range(7):
            code_copy(k, i).wait_send()
    pltpu.make_async_remote_copy(
        src_ref=codes.at[1 - mine, 7], dst_ref=landed.at[9], send_sem=rs_send.at[1 - mine, 7], recv_sem=rs_recv.at[9],
        device_id=(tm, (1 - lo) * 8 + z), device_id_type=MESH,
    ).wait_send()
    for copy in sends:
        copy.wait_send()

    @pl.when(tm > 0)
    def _():
        for half in range(2):
            edge_copy(half).wait_send()


def body(snapshots, spod_modes, freq_index, seg_offsets):
    bf16, f32 = jnp.bfloat16, jnp.float32
    vmem = pltpu.VMEM
    dma = pltpu.SemaphoreType.DMA
    return pl.pallas_call(
        kernel,
        out_shape=vmem((F // 16, 2, M, S), f32),
        in_specs=[
            pl.BlockSpec(memory_space=pltpu.SMEM),
            pl.BlockSpec(memory_space=pl.ANY),
            pl.BlockSpec(memory_space=pl.ANY),
            pl.BlockSpec(memory_space=vmem),
        ],
        out_specs=pl.BlockSpec(memory_space=vmem),
        scratch_shapes=[
            vmem((T, R), bf16),
            vmem((2, HALF, R), bf16),
            vmem((2, HALF, T + L), bf16),
            vmem((2, HALF, T + L), bf16),
            vmem((T + L, S), bf16),
            vmem((T + L, S), bf16),
            vmem((2, HALF, L), f32),
            vmem((2, HALF, L), f32),
            vmem((L, S), f32),
            vmem((BLOCK, S), f32),
            vmem((BLOCK, S), f32),
            vmem((2, HALF, S), f32),
            vmem((2, 8, 4 * BLOCK + 16, 128), jnp.int16),
            vmem((10, 4 * BLOCK + 16, 128), jnp.int16),
            vmem((2, 3, 4 * BLOCK + 16, 128), jnp.int16),
            vmem((F // 16, 2, M, R), bf16),
            vmem((BLOCK, S), f32),
            vmem((2, HALF + 32, L), jnp.int16),
            vmem((2, HALF + 32, L), jnp.int16),
            dma, dma,
            dma((15,)), dma((16,)),
            dma((2,)), dma((2,)),
            dma((2, 8)), dma((10,)), dma((2, 3)),
        ],
        compiler_params=pltpu.CompilerParams(
            collective_id=0, has_side_effects=True, vmem_limit_bytes=56 * 1024 * 1024
        ),
        cost_estimate=pl.CostEstimate(flops=8 * 10**9, bytes_accessed=10**7, transcendentals=0),
    )(freq_index, snapshots, spod_modes, seg_offsets.reshape(1, S))


def solution(mesh):
    placed = (P("tm", "rows"), P("tm", None, None, "rows"), P(), P("tm"))
    return jax.shard_map(
        body, mesh=mesh, in_specs=placed, out_specs=P("rows", None, None, "tm"), check_vma=False
    )
```
